512 devices in a mesh: grp: 8 (over y_hi, core), dp: 64 (over y_lo, z, x).
Axes of the slice: x: 4, y: 8 (y_hi: 4, y_lo: 2; y = y_hi * 2 + y_lo), z: 8, core: 2. Of those that a mesh axis runs over, the one named last changes fastest.
Arguments:
- teacher_in: bfloat16 [1024, 4096], P('grp', 'dp'), may hold values from -6 to 6
- norm_gain: bfloat16 [4096], P('dp'), may hold values from 0.25 to 1.75
- gate_w: bfloat16 [4096, 4096], P(None, 'dp'), may hold values from -0.09375 to 0.09375
- up_w: bfloat16 [4096, 4096], P(None, 'dp'), may hold values from -0.09375 to 0.09375
- down_w: bfloat16 [4096, 4096], P('dp'), may hold values from -0.09375 to 0.09375
- prev_rows: bfloat16 [4096, 4096], P('dp', 'grp'), may hold values from -6 to 6
- student_in: bfloat16 [65536, 768], P('dp'), may hold values from -6 to 6
- student_w: bfloat16 [768, 4096], P(None, 'grp'), may hold values from -0.21875 to 0.21875
- target_rows: int32 [64, 64, 16], replicated, may hold values from 0 to 63
- counts: int32 [64], replicated, may hold values from 1 to 1024, 33280 in all
Outputs:
- teacher_out: bfloat16 [1024, 4096], P('grp', 'dp')
- grad_w: float32 [768, 4096], P('dp', 'grp')
- loss: float32 [], replicated
The draws below stay inside these ranges and needn't reach their ends.
Inputs may be any that keep to these rules, and one draw needn't show every extreme that they name: Student token s * 16 + j of index h of dp uses row target_rows[h, s, j] of the rows held by index s of dp.
All inputs are finite; a program needn't handle non-finite values.
Results may differ from the reference program's by a relative error of at most 0.0051.
Values may be sent and summed in bfloat16 or wider, within the bound.
A program may use at most 64 MiB of HBM per device.

```python
import math
import jax
import jax.numpy as jnp
import numpy as np
from jax import lax

D_T = 4096
FF = 4096
D_S = 768
TROWS = 64
S_DEV = 1024
CAPP = 16
TOKENS_T = 1024
ROWS_T = 4096
TOKENS_S = 65536
N_DP = 64


def touch_ends(array, stream_key, least, top_value):
    place = [jax.random.randint(jax.random.fold_in(stream_key, axis), (), 0, length) for axis, length in enumerate(array.shape)]
    main_axis = array.shape.index(max(array.shape))
    beside = place[:main_axis] + [(place[main_axis] + 1) % array.shape[main_axis]] + place[main_axis + 1:]
    return array.at[tuple(place)].set(least).at[tuple(beside)].set(top_value)


def steps_of(own_key, extent, split, low, top_value):
    level, own = 1.0, jax.random.fold_in(own_key, 6)
    for position, shards_of in split:
        steps = jnp.exp(jax.random.uniform(jax.random.fold_in(own, position), (shards_of,), jnp.float32, low / len(split), top_value / len(split)))
        level = level * jnp.repeat(steps, extent[position] // shards_of).reshape([-1 if axis == position else 1 for axis in range(len(extent))])
    return level


def split_up(amount, total, bound, skew):
    weights = [(1 << 20) // math.isqrt(rank ** skew) + 1 for rank in range(2, amount + 1)]
    rest, holding = total - bound - (amount - 1), [1] * (amount - 1)
    while rest > 0:
        free = [i for i in range(amount - 1) if holding[i] < bound]
        whole, remaining = sum([weights[i] for i in free]), rest
        for i in free:
            more = min(bound - holding[i], max(1, remaining * weights[i] // whole), rest)
            holding[i] = holding[i] + more
            rest = rest - more
    return np.array([bound] + holding)


def ragged_sizes(key, amount, total, bound, lean):
    if amount == 2:
        one = jax.random.randint(key, (), max(1, total - bound), min(bound, total - 1) + 1)
        return jnp.stack([one, total - one])
    tallies = jnp.asarray(split_up(amount, total, bound, lean), jnp.int32)
    twos = (amount - 1) // 2
    donor, receiver = tallies[1:1 + 2 * twos:2], tallies[2:2 + 2 * twos:2]
    room = jnp.minimum(donor - 1, bound - receiver)
    shifted = jax.random.randint(jax.random.fold_in(key, 1), (twos,), 0, 1 << 20) % (room + 1)
    tallies = tallies.at[1:1 + 2 * twos:2].set(donor - shifted).at[2:2 + 2 * twos:2].set(receiver + shifted)
    return tallies[jax.random.permutation(jax.random.fold_in(key, 2), amount)]


def bell_draw(rng, shape, spread, reach, split=(), held_as=jnp.bfloat16):
    values = jax.random.normal(rng, shape, jnp.float32) * spread
    if len(split) > 0:
        values = steps_of(rng, shape, split, -0.22, 0.18) * values
    return jnp.clip(values, min=-reach, max=reach).astype(held_as)


def setup_inputs(seed: int = 0) -> dict:
    streams_of = jax.random.split(jax.random.key(seed), 11)
    teacher_in = bell_draw(streams_of[0], (TOKENS_T, D_T), 1.0, 6.0, ((0, 8), (1, 64)))
    norm_gain = jnp.clip(1.0 + 0.15 * jax.random.normal(streams_of[1], (D_T,), jnp.float32), 0.25, 1.75).astype(jnp.bfloat16)
    gate_w = bell_draw(streams_of[2], (D_T, FF), D_T ** -0.5, 0.09375, ((1, 64),))
    up_w = bell_draw(streams_of[3], (D_T, FF), D_T ** -0.5, 0.09375, ((1, 64),))
    down_w = bell_draw(streams_of[4], (FF, D_T), FF ** -0.5, 0.09375, ((0, 64),))
    prev_rows = bell_draw(streams_of[5], (ROWS_T, D_T), 1.0, 6.0, ((0, 64), (1, 8)))
    student_in = bell_draw(streams_of[6], (TOKENS_S, D_S), 1.0, 6.0, ((0, 64),))
    student_w = bell_draw(streams_of[7], (D_S, D_T), D_S ** -0.5, 0.21875, ((1, 8),))
    target_rows = touch_ends(jax.random.randint(streams_of[8], (N_DP, N_DP, CAPP), 0, TROWS), jax.random.fold_in(streams_of[8], 1), 0, TROWS - 1).astype(jnp.int32)
    counts = ragged_sizes(streams_of[9], N_DP, N_DP * S_DEV // 2 + S_DEV // 2, S_DEV, 1).astype(jnp.int32)
    return {"teacher_in": teacher_in, "norm_gain": norm_gain, "gate_w": gate_w, "up_w": up_w, "down_w": down_w, "prev_rows": prev_rows, "student_in": student_in, "student_w": student_w, "target_rows": target_rows, "counts": counts}


def reference(teacher_in, norm_gain, gate_w, up_w, down_w, prev_rows, student_in, student_w, target_rows, counts):
    xf = teacher_in.astype(jnp.float32)
    scale = jax.lax.rsqrt(lax.optimization_barrier(jnp.mean(xf * xf, axis=-1, keepdims=True)) + 1e-05)
    normed = (xf * scale * norm_gain.astype(jnp.float32)).astype(jnp.bfloat16)
    gate = jnp.dot(normed, gate_w, preferred_element_type=jnp.float32)
    up = jnp.dot(normed, up_w, preferred_element_type=jnp.float32)
    hidden = (jax.nn.silu(gate) * up).astype(jnp.bfloat16)
    mix = jnp.dot(hidden, down_w, preferred_element_type=jnp.float32)
    teacher_out = (xf + mix).astype(jnp.bfloat16)
    offsets = (jnp.arange(N_DP, dtype=jnp.int32) * TROWS)[None, :, None]
    index = (target_rows + offsets).astype(jnp.int32).reshape(-1)
    teach = jnp.take(prev_rows, index, axis=0).astype(jnp.float32)
    pred = jnp.dot(student_in, student_w, preferred_element_type=jnp.float32)
    pp = lax.optimization_barrier(jnp.sum(pred * pred, axis=-1)) + 1e-06
    tt = lax.optimization_barrier(jnp.sum(teach * teach, axis=-1)) + 1e-06
    pt = lax.optimization_barrier(jnp.sum(pred * teach, axis=-1))
    inv = jax.lax.rsqrt(pp * tt)
    cos = pt * inv
    valid = (jnp.arange(S_DEV, dtype=jnp.int32)[None, :] < counts[:, None]).reshape(-1).astype(jnp.float32)
    loss = jnp.sum(valid * (1.0 - cos)) / jnp.sum(counts).astype(jnp.float32)
    weight = valid * (D_T / S_DEV)
    dpred = ((weight * pt * inv / pp)[:, None] * pred - (weight * inv)[:, None] * teach).astype(jnp.bfloat16)
    grad_w = jnp.dot(student_in.T, dpred, preferred_element_type=jnp.float32)
    return (teacher_out, grad_w, loss)
```

```python
import functools

import jax
import jax.numpy as jnp
from jax import lax
from jax.experimental import pallas as pl
from jax.experimental.pallas import tpu as pltpu
from jax.sharding import PartitionSpec as P

NY = 2
CAP = 16
MESH = pl.DeviceIdType.MESH
F32 = jnp.float32
BF16 = jnp.bfloat16

XG_Z, SS_Z, ROWS_Z, XG_P, SS_P, ROWS_P, STATS, MIX_P, MIX_Z, GRAD_P, GRAD_Z, LOSS_P, LOSS_Z = range(13)
STAGES = 13


def dot(a, b, ca, cb):
    return lax.dot_general(a, b, (((ca,), (cb,)), ((), ())), preferred_element_type=F32)


def iota(shape, axis):
    return lax.broadcasted_iota(jnp.int32, shape, axis)


def kernel(
    nz, nx,
    tin, gain, rows, gate_h, up_h, down_h, x_h, w_h, tr_h, counts,
    tout, gout, loss_out,
    gu, down, xv, wv, tr, xf, xn, ss1, ss2, ssz, ssp, rz, sel, tts, tta, wt, xt, pred, stat, stats, dpt,
    grad, gs, gr, gacc, gzf, gz, gzr, loss1, loss2, lossp, lossz, mix, mixb, mr, mzf, mz, mzr,
    send, recv, local,
):
    nk = NY * nx
    ndp = nk * nz
    groups = lax.axis_size("grp")
    g, dp = lax.axis_index("grp"), lax.axis_index("dp")
    y, z, x = dp // (nz * nx), (dp // nx) % nz, dp % nx
    me = y * nx + x
    nfeat, ntok = tin.shape
    trows, width = rows.shape
    ds = wv.shape[0]
    cap_z = nz * CAP
    tokens = cap_z * nk
    part = ds // nk
    out_rows = part // nz

    def z_peer(d):
        zz = (z + d) % nz
        return zz, (g, (y * nz + zz) * nx + x)

    def p_peer(d):
        yy, xx = (y + d // nx) % NY, (x + d % nx) % nx
        return yy, xx, (g, (yy * nz + z) * nx + xx)

    def p_source(d):
        return (y + NY - d // nx) % NY, (x + nx - d % nx) % nx

    def g_peer(d):
        return ((g + d) % groups, dp)

    def rcopy(src, dst, stage, d, device):
        return pltpu.make_async_remote_copy(
            src_ref=src, dst_ref=dst, send_sem=send.at[stage, d], recv_sem=recv.at[stage, d],
            device_id=device, device_id_type=MESH,
        )

    started = []

    def start(*args):
        copy = rcopy(*args)
        copy.start()
        started.append(copy)

    def arrived(ref, stage, d):
        rcopy(ref, ref, stage, d, z_peer(1)[1]).wait_recv()

    loads = []

    def load(src, dst):
        copy = pltpu.make_async_copy(src, dst, local.at[len(loads)])
        copy.start()
        loads.append(copy)

    for yy in range(NY):
        load(tr_h.at[yy, z], tr.at[pl.ds(yy * nx, nx)])
    load(w_h, wv)
    for d in range(nk):
        yy, xx = p_source(d)
        load(x_h.at[yy, :, xx], xv.at[d])
    load(gate_h, gu.at[pl.ds(0, nfeat)])
    load(up_h, gu.at[pl.ds(nfeat, nfeat)])
    load(down_h, down)

    rz[0] = rows[...]
    xin = tin[...].astype(F32)
    eye = iota((nfeat, nfeat), 0) == iota((nfeat, nfeat), 1)
    gain_col = jnp.sum(jnp.where(eye, gain[...].astype(F32), 0.0), axis=1, keepdims=True)
    xf[0, 0] = (xin * gain_col).astype(BF16)
    ss1[...] = jnp.sum((xin * xin).reshape(nfeat // 8, 8, ntok), axis=0)

    barrier = pltpu.get_barrier_semaphore()
    peers = (
        [z_peer(d)[1] for d in range(1, nz)]
        + [p_peer(d)[2] for d in range(1, nk)]
        + [g_peer(d) for d in range(1, groups)]
    )
    for device in peers:
        pl.semaphore_signal(barrier, inc=1, device_id=device, device_id_type=MESH)
    pl.semaphore_wait(barrier, len(peers))

    for d in range(1, nz):
        start(rz.at[0], rz.at[d], ROWS_Z, d, z_peer(d)[1])
    for d in range(1, nz):
        start(xf.at[0, 0], xf.at[0, d], XG_Z, d, z_peer(d)[1])
        start(ss1, ssz.at[d], SS_Z, d, z_peer(d)[1])

    for copy in loads[:NY]:
        copy.wait()
    pick = (iota((ndp, cap_z), 0) == (y * nz + lax.shift_right_logical(iota((ndp, cap_z), 1), 4)) * nx + x)
    slots = dot(tr[...].reshape(nk * CAP, ndp).astype(F32).astype(BF16), pick.astype(F32).astype(BF16), 1, 0)
    mine = iota((nk, CAP, cap_z), 1) == (iota((nk, CAP, cap_z), 2) & (CAP - 1))
    target = jnp.sum(jnp.where(mine, slots.reshape(nk, CAP, cap_z), 0.0), axis=1)
    slot_z = (z + nz - lax.shift_right_logical(iota((nk, cap_z), 1), 4)) & (nz - 1)
    sel[...] = target.astype(jnp.int32) + slot_z * trows

    for copy in loads[NY : NY + 1 + nk]:
        copy.wait()
    wt[...] = wv[...].T
    for k in range(nk):
        p = dot(wt[...], xv[k].reshape(cap_z, ds), 1, 1)
        pred[k] = p
        stat[0, k : k + 1, :] = jnp.sum(p * p, axis=0, keepdims=True)

    for d in range(1, nz):
        arrived(rz.at[d], ROWS_Z, d)
    rz_t = rz[...].reshape(nz * trows, width).T
    row_of = iota((nz * trows, cap_z), 0)
    for d in list(range(1, nk)) + [0]:
        yy, xx, device = p_peer(d)
        onehot = (row_of == sel[pl.ds(yy * nx + xx, 1), :]).astype(F32).astype(BF16)
        picked = dot(rz_t, onehot, 1, 0).astype(BF16)
        if d == 0:
            tta[0] = picked
        else:
            tts[d] = picked
            start(tts.at[d], tta.at[d], ROWS_P, d, device)

    for d in range(1, nz):
        arrived(xf.at[0, d], XG_Z, d)
        arrived(ssz.at[d], SS_Z, d)
    squares = ss1[...]
    for d in range(1, nz):
        squares += ssz[d]
    ss2[...] = squares
    for d in range(1, nk):
        device = p_peer(d)[2]
        start(xf.at[0], xf.at[d], XG_P, d, device)
        start(ss2, ssp.at[d], SS_P, d, device)

    r = iota((ds, 1), 0).astype(F32)
    rk = jnp.floor((r + 0.5) / part)
    rz_ = jnp.floor((r - rk * part + 0.5) / out_rows)
    ry = jnp.floor((rk + 0.5) / nx)
    column = ((ry * nz + rz_) * nx + (rk - ry * nx)) * out_rows + (r - rk * part - rz_ * out_rows)
    order = (column == iota((ds, ds), 1).astype(F32)).astype(F32).astype(BF16)
    for k in range(nk):
        xt[:, k * cap_z : (k + 1) * cap_z] = dot(order, xv[k].reshape(cap_z, ds), 1, 1).astype(BF16)

    for d in range(nk):
        if d:
            arrived(tta.at[d], ROWS_P, d)
        t = tta[d].astype(F32)
        stat[1, d : d + 1, :] = jnp.sum(t * t, axis=0, keepdims=True)
        stat[2, d : d + 1, :] = jnp.sum(t * pred[d], axis=0, keepdims=True)
    for d in range(1, groups):
        start(stat, stats.at[d], STATS, d, g_peer(d))

    for d in range(1, nk):
        arrived(xf.at[d], XG_P, d)
        arrived(ssp.at[d], SS_P, d)
    for d in range(1, nk):
        squares += ssp[d]
    total = jnp.sum(squares, axis=0, keepdims=True)
    scale = lax.rsqrt(total * (1.0 / (ndp * nfeat)) + 1e-05)
    for copy in loads[NY + 1 + nk :]:
        copy.wait()
    for d in range(nk):
        yy, xx = p_source(d)
        for dz in range(nz):
            xn[yy * nz + (z + nz - dz) % nz, xx] = xf[d, dz]
    h = dot(gu[...], xn[...].reshape(ndp * nfeat, ntok), 1, 0)
    gate, up = h[:nfeat] * scale, h[nfeat:] * scale
    hidden = (gate * jax.nn.sigmoid(gate) * up).astype(BF16)
    per_y = nz * nx * nfeat
    for yy in range(NY):
        m = dot(down[:, yy * per_y : (yy + 1) * per_y], hidden, 0, 0).reshape(nz, nx, nfeat, ntok)
        mix[pl.ds(yy * nz, nz)] = m
        for xx in range(nx):
            mixb[xx, pl.ds(yy * nz, nz)] = m[:, xx].astype(BF16)
    for d in range(1, nk):
        yy, xx, device = p_peer(d)
        start(mixb.at[xx, pl.ds(yy * nz, nz)], mr.at[d], MIX_P, d, device)

    for d in range(1, groups):
        arrived(stats.at[d], STATS, d)
    sums = stat[...]
    for d in range(1, groups):
        sums += stats[d]
    pp, tt, pt = sums[0] + 1e-06, sums[1] + 1e-06, sums[2]
    inv = lax.rsqrt(pp * tt)
    kk, lane = iota((nk, cap_z), 0), iota((nk, cap_z), 1)
    ky = (y + NY - lax.shift_right_logical(kk, nx.bit_length() - 1)) & (NY - 1)
    kx = (x + nx - (kk & (nx - 1))) & (nx - 1)
    source = (ky * nz + lax.shift_right_logical(lane, 4)) * nx + kx
    valid = (source * CAP + (lane & (CAP - 1)) < counts[dp]).astype(F32)
    weight = valid * (ndp * nfeat / tokens)
    count = lax.fori_loop(0, ndp, lambda i, c: c + counts[i], jnp.int32(0))
    loss1[...] = valid * (1.0 - pt * inv)
    for d in range(1, nk):
        start(loss1, lossp.at[d], LOSS_P, d, p_peer(d)[2])
    a, b = weight * pt * inv / pp, weight * inv
    for k in range(nk):
        dpt[:, k * cap_z : (k + 1) * cap_z] = (
            a[k : k + 1] * pred[k] - b[k : k + 1] * tta[k].astype(F32)
        ).astype(BF16)
    gw = dot(xt[...], dpt[...], 1, 1).reshape(nk, part, width)
    grad[...] = gw
    gs[...] = gw.astype(BF16)
    for d in range(1, nk):
        yy, xx, device = p_peer(d)
        start(gs.at[yy * nx + xx], gr.at[d], GRAD_P, d, device)

    for d in range(1, nk):
        arrived(mr.at[d], MIX_P, d)
    m = mix[pl.ds(y * nz, nz), x]
    for d in range(1, nk):
        m += mr[d].astype(F32)
    mzf[...] = m
    mz[...] = m.astype(BF16)
    for d in range(1, nz):
        zz, device = z_peer(d)
        start(mz.at[zz], mzr.at[d], MIX_Z, d, device)

    for d in range(1, nk):
        arrived(lossp.at[d], LOSS_P, d)
    part_loss = loss1[...]
    for d in range(1, nk):
        part_loss += lossp[d]
    loss2[...] = part_loss
    for d in range(1, nz):
        start(loss2, lossz.at[d], LOSS_Z, d, z_peer(d)[1])

    for d in range(1, nk):
        arrived(gr.at[d], GRAD_P, d)
    acc = grad[me]
    for d in range(1, nk):
        acc += gr[d].astype(F32)
    gacc[pl.ds(0, part)] = acc
    gacc[pl.ds(part, 16)] = jnp.zeros((16, width), F32)
    for zz in range(nz):
        piece = gacc[pl.ds(zz * out_rows, 16)]
        gzf[zz] = piece
        gz[zz] = piece.astype(BF16)
    for d in range(1, nz):
        zz, device = z_peer(d)
        start(gz.at[zz], gzr.at[d], GRAD_Z, d, device)

    m = xin + mzf[z]
    for d in range(1, nz):
        arrived(mzr.at[d], MIX_Z, d)
        m += mzr[d].astype(F32)
    tout[...] = m.astype(BF16)

    for d in range(1, nz):
        arrived(lossz.at[d], LOSS_Z, d)
        part_loss += lossz[d]
    loss_out[0, 0] = jnp.sum(part_loss) / count.astype(F32)

    acc = gzf[z]
    for d in range(1, nz):
        arrived(gzr.at[d], GRAD_Z, d)
        acc += gzr[d].astype(F32)
    gout[...] = acc[:out_rows]

    for copy in started:
        copy.wait_send()


def on_device(
    nz, nx, teacher_in, norm_gain, gate_w, up_w, down_w, prev_rows, student_in, student_w, target_rows, counts
):
    nk = NY * nx
    ndp = nk * nz
    ntok, nfeat = teacher_in.shape
    trows, width = prev_rows.shape
    s_dev, ds = student_in.shape
    groups = lax.axis_size("grp")
    cap_z = nz * CAP
    part = ds // nk
    out_rows = part // nz
    d_model = ndp * nfeat
    vm = pl.BlockSpec(memory_space=pltpu.VMEM)
    hbm = pl.BlockSpec(memory_space=pl.ANY)
    sm = pl.BlockSpec(memory_space=pltpu.SMEM)
    v = pltpu.VMEM
    scratch = [
        v((2 * nfeat, d_model), BF16),
        v((nfeat, d_model), BF16),
        v((nk, nz, CAP, ds), BF16),
        v((ds, width), BF16),
        v((nk, CAP, ndp), jnp.int32),
        v((nk, nz, nfeat, ntok), BF16),
        v((NY * nz, nx, nfeat, ntok), BF16),
        v((8, ntok), F32),
        v((8, ntok), F32),
        v((nz, 8, ntok), F32),
        v((nk, 8, ntok), F32),
        v((nz, trows, width), BF16),
        v((nk, cap_z), jnp.int32),
        v((nk, width, cap_z), BF16),
        v((nk, width, cap_z), BF16),
        v((width, ds), BF16),
        v((ds, s_dev), BF16),
        v((nk, width, cap_z), F32),
        v((3, nk, cap_z), F32),
        v((groups, 3, nk, cap_z), F32),
        v((width, s_dev), BF16),
        v((nk, part, width), F32),
        v((nk, part, width), BF16),
        v((nk, part, width), BF16),
        v((part + 16, width), F32),
        v((nz, 16, width), F32),
        v((nz, 16, width), BF16),
        v((nz, 16, width), BF16),
        v((nk, cap_z), F32),
        v((nk, cap_z), F32),
        v((nk, nk, cap_z), F32),
        v((nz, nk, cap_z), F32),
        v((NY * nz, nx, nfeat, ntok), F32),
        v((nx, NY * nz, nfeat, ntok), BF16),
        v((nk, nz, nfeat, ntok), BF16),
        v((nz, nfeat, ntok), F32),
        v((nz, nfeat, ntok), BF16),
        v((nz, nfeat, ntok), BF16),
        pltpu.SemaphoreType.DMA((STAGES, max(nk, nz, groups))),
        pltpu.SemaphoreType.DMA((STAGES, max(nk, nz, groups))),
        pltpu.SemaphoreType.DMA((NY + 4 + nk,)),
    ]
    tout, gout, loss = pl.pallas_call(
        functools.partial(kernel, nz, nx),
        out_shape=(
            jax.ShapeDtypeStruct((nfeat, ntok), BF16),
            jax.ShapeDtypeStruct((out_rows, width), F32),
            jax.ShapeDtypeStruct((1, 1), F32),
        ),
        in_specs=[vm, vm, vm, hbm, hbm, hbm, hbm, hbm, hbm, sm],
        out_specs=(vm, vm, sm),
        scratch_shapes=scratch,
        compiler_params=pltpu.CompilerParams(
            collective_id=0, has_side_effects=True, vmem_limit_bytes=52 * 1024 * 1024
        ),
        name="distill",
    )(
        teacher_in.T,
        norm_gain.reshape(1, nfeat),
        prev_rows,
        gate_w.T,
        up_w.T,
        down_w,
        student_in.reshape(NY, nz, nx, CAP, ds),
        student_w,
        target_rows.transpose(0, 2, 1).reshape(NY, nz, nx, CAP, ndp),
        counts,
    )
    return tout.T, gout, loss.reshape(())


def solution(mesh):
    in_specs = (
        P("grp", "dp"),
        P("dp"),
        P(None, "dp"),
        P(None, "dp"),
        P("dp", None),
        P("dp", "grp"),
        P("dp", None),
        P(None, "grp"),
        P(),
        P(),
    )
    out_specs = (P("grp", "dp"), P("dp", "grp"), P())
    nx = 4
    nz = mesh.shape["dp"] // (NY * nx)
    return jax.shard_map(
        functools.partial(on_device, nz, nx), mesh=mesh, in_specs=in_specs, out_specs=out_specs, check_vma=False
    )
```

```python
import functools

import jax
import jax.numpy as jnp
from jax import lax
from jax.experimental import pallas as pl
from jax.experimental.pallas import tpu as pltpu
from jax.sharding import PartitionSpec as P

NY = 2
CAP = 16
MESH = pl.DeviceIdType.MESH
F32 = jnp.float32
BF16 = jnp.bfloat16

(
    XA_P, XA_Z, XB_Z, XB_P, SS_Z, SS_P, ROWS_Z0, ROWS_Z1, ROWS_P0, ROWS_P1, STATS,
    MA_P, MA_Z, MB_Z, MB_P, GRAD_P, GRAD_Z, LOSS_P, LOSS_Z,
) = range(19)
STAGES = 19


def dot(a, b, ca, cb):
    return lax.dot_general(a, b, (((ca,), (cb,)), ((), ())), preferred_element_type=F32)


def iota(shape, axis):
    return lax.broadcasted_iota(jnp.int32, shape, axis)


def kernel(
    nz, nx,
    tin, gain, rows, gate_h, up_h, down_h, x_h, w_h, tr_h, counts,
    tout, gout, loss_out,
    gu, down, xv, wv, tr, xa, xb, xn, ss1, ss2, ssz, ssp, rz, hot, tts, tta, wt, xt, pred, stat, stats, dpt,
    grad, gs, gr, gacc, gzf, gz, gzr, loss1, loss2, lossp, lossz,
    mix, mixa, mixb, mra, mrb, mfa, mfb, m2a, m2b, mr2a, mr2b,
    send, recv, local,
):
    nk = NY * nx
    ndp = nk * nz
    groups = lax.axis_size("grp")
    g, dp = lax.axis_index("grp"), lax.axis_index("dp")
    y, z, x = dp // (nz * nx), (dp // nx) % nz, dp % nx
    me = y * nx + x
    nfeat, ntok = tin.shape
    trows, width = rows.shape
    ds = wv.shape[0]
    cap_z = nz * CAP
    tokens = cap_z * nk
    part = ds // nk
    out_rows = part // nz
    half, fh = width // 2, nfeat // 2

    def z_peer(d):
        zz = (z + d) % nz
        return zz, (g, (y * nz + zz) * nx + x)

    def p_peer(d):
        yy, xx = (y + d // nx) % NY, (x + d % nx) % nx
        return yy, xx, (g, (yy * nz + z) * nx + xx)

    def p_source(d):
        return (y + NY - d // nx) % NY, (x + nx - d % nx) % nx

    def g_peer(d):
        return ((g + d) % groups, dp)

    def rcopy(src, dst, stage, d, device):
        return pltpu.make_async_remote_copy(
            src_ref=src, dst_ref=dst, send_sem=send.at[stage, d], recv_sem=recv.at[stage, d],
            device_id=device, device_id_type=MESH,
        )

    started = []

    def start(*args):
        copy = rcopy(*args)
        copy.start()
        started.append(copy)

    def arrived(ref, stage, d):
        rcopy(ref, ref, stage, d, z_peer(1)[1]).wait_recv()

    loads = []

    def load(src, dst):
        copy = pltpu.make_async_copy(src, dst, local.at[len(loads)])
        copy.start()
        loads.append(copy)

    for yy in range(NY):
        load(tr_h.at[yy, z], tr.at[pl.ds(yy * nx, nx)])
    load(w_h, wv)
    for d in range(nk):
        yy, xx = p_source(d)
        load(x_h.at[yy, :, xx], xv.at[d])
    load(gate_h, gu.at[pl.ds(0, nfeat)])
    load(up_h, gu.at[pl.ds(nfeat, nfeat)])
    load(down_h, down)

    for c in range(2):
        rz[c, 0] = rows[:, c * half : (c + 1) * half]
    xin = tin[...].astype(F32)
    eye = iota((nfeat, nfeat), 0) == iota((nfeat, nfeat), 1)
    gain_col = jnp.sum(jnp.where(eye, gain[...].astype(F32), 0.0), axis=1, keepdims=True)
    xg = (xin * gain_col).astype(BF16)
    xa[0, 0] = xg[:fh]
    xb[0, 0] = xg[fh:]
    squares = jnp.sum((xin * xin).reshape(nfeat // 8, 8, ntok), axis=0)
    ss1[...] = squares

    barrier = pltpu.get_barrier_semaphore()
    peers = (
        [z_peer(d)[1] for d in range(1, nz)]
        + [p_peer(d)[2] for d in range(1, nk)]
        + [g_peer(d) for d in range(1, groups)]
    )
    for device in peers:
        pl.semaphore_signal(barrier, inc=1, device_id=device, device_id_type=MESH)
    pl.semaphore_wait(barrier, len(peers))

    relay = nz == 8
    for c in range(2):
        for d in (2, 6, 1, 7) if relay else range(1, nz):
            start(rz.at[c, 0], rz.at[c, d], ROWS_Z0 + c, d, z_peer(d)[1])
    for d in range(1, nk):
        start(xa.at[0, 0], xa.at[0, d], XA_P, d, p_peer(d)[2])
    for d in range(1, nz):
        start(xb.at[0, 0], xb.at[0, d], XB_Z, d, z_peer(d)[1])
        start(ss1, ssz.at[d], SS_Z, d, z_peer(d)[1])

    for copy in loads[:NY]:
        copy.wait()
    pick = (iota((ndp, cap_z), 0) == (y * nz + lax.shift_right_logical(iota((ndp, cap_z), 1), 4)) * nx + x)
    slots = dot(tr[...].reshape(nk * CAP, ndp).astype(F32).astype(BF16), pick.astype(F32).astype(BF16), 1, 0)
    mine = iota((nk, CAP, cap_z), 1) == (iota((nk, CAP, cap_z), 2) & (CAP - 1))
    target = jnp.sum(jnp.where(mine, slots.reshape(nk, CAP, cap_z), 0.0), axis=1)
    slot_z = (z + nz - lax.shift_right_logical(iota((nk, cap_z), 1), 4)) & (nz - 1)
    sel = target.astype(jnp.int32) + slot_z * trows
    row_of = iota((nz * trows, cap_z), 0)
    for k in range(nk):
        hot[k] = (row_of == sel[k : k + 1]).astype(F32).astype(BF16)

    if relay:
        low, high = pl.ds(0, trows // 2), pl.ds(trows // 2, trows // 2)
        for c in range(2):
            stage = ROWS_Z0 + c
            arrived(rz.at[c, 2], stage, 2)
            start(rz.at[c, 2, low], rz.at[c, 4, low], stage, 4, z_peer(2)[1])
            start(rz.at[c, 2], rz.at[c, 3], stage, 3, z_peer(1)[1])
            arrived(rz.at[c, 6], stage, 6)
            start(rz.at[c, 6, high], rz.at[c, 4, high], stage, 0, z_peer(6)[1])
            start(rz.at[c, 6], rz.at[c, 5], stage, 5, z_peer(7)[1])

    for d in range(1, nk):
        arrived(xa.at[0, d], XA_P, d)
    for d in range(1, nz):
        start(xa.at[0], xa.at[d], XA_Z, d, z_peer(d)[1])

    for copy in loads[NY : NY + 1 + nk]:
        copy.wait()
    wt[...] = wv[...].T
    for k in range(nk):
        p = dot(wt[...], xv[k].reshape(cap_z, ds), 1, 1)
        pred[k] = p
        stat[0, k : k + 1, :] = jnp.sum(p * p, axis=0, keepdims=True)

    for c in range(2):
        stage = ROWS_Z0 + c
        if relay:
            for d in (1, 7, 3, 5):
                arrived(rz.at[c, d], stage, d)
            arrived(rz.at[c, 4, low], stage, 4)
            arrived(rz.at[c, 4, high], stage, 0)
        else:
            for d in range(1, nz):
                arrived(rz.at[c, d], stage, d)
        rz_t = rz[c].reshape(nz * trows, half).T
        for d in list(range(1, nk)) + [0]:
            yy, xx, device = p_peer(d)
            picked = dot(rz_t, hot[yy * nx + xx], 1, 0).astype(BF16)
            if d == 0:
                tta[c, 0] = picked
            else:
                tts[c, d] = picked
                start(tts.at[c, d], tta.at[c, d], ROWS_P0 + c, d, device)

    for d in range(1, nz):
        arrived(xb.at[0, d], XB_Z, d)
        arrived(ssz.at[d], SS_Z, d)
        squares += ssz[d]
    ss2[...] = squares
    for d in range(1, nk):
        device = p_peer(d)[2]
        start(xb.at[0], xb.at[d], XB_P, d, device)
        start(ss2, ssp.at[d], SS_P, d, device)

    r = iota((ds, 1), 0).astype(F32)
    rk = jnp.floor((r + 0.5) / part)
    rz_ = jnp.floor((r - rk * part + 0.5) / out_rows)
    ry = jnp.floor((rk + 0.5) / nx)
    column = ((ry * nz + rz_) * nx + (rk - ry * nx)) * out_rows + (r - rk * part - rz_ * out_rows)
    order = (column == iota((ds, ds), 1).astype(F32)).astype(F32).astype(BF16)
    for k in range(nk):
        xt[:, k * cap_z : (k + 1) * cap_z] = dot(order, xv[k].reshape(cap_z, ds), 1, 1).astype(BF16)

    for d in range(nk):
        tt_sum = pt_sum = 0.0
        for c in range(2):
            if d:
                arrived(tta.at[c, d], ROWS_P0 + c, d)
            t = tta[c, d].astype(F32)
            tt_sum += jnp.sum(t * t, axis=0, keepdims=True)
            pt_sum += jnp.sum(t * pred[d, c * half : (c + 1) * half], axis=0, keepdims=True)
        stat[1, d : d + 1, :] = tt_sum
        stat[2, d : d + 1, :] = pt_sum
    for d in range(1, groups):
        start(stat, stats.at[d], STATS, d, g_peer(d))

    for d in range(1, nk):
        arrived(ssp.at[d], SS_P, d)
        squares += ssp[d]
        arrived(xb.at[d], XB_P, d)
    for d in range(1, nz):
        arrived(xa.at[d], XA_Z, d)
    total = jnp.sum(squares, axis=0, keepdims=True)
    scale = lax.rsqrt(total * (1.0 / (ndp * nfeat)) + 1e-05)
    for copy in loads[NY + 1 + nk :]:
        copy.wait()
    for d in range(nk):
        yy, xx = p_source(d)
        for dz in range(nz):
            place = yy * nz + (z + nz - dz) % nz
            xn[place, xx, :fh] = xa[dz, d]
            xn[place, xx, fh:] = xb[d, dz]
    h = dot(gu[...], xn[...].reshape(ndp * nfeat, ntok), 1, 0)
    gate, up = h[:nfeat] * scale, h[nfeat:] * scale
    hidden = (gate * jax.nn.sigmoid(gate) * up).astype(BF16)
    per_y = nz * nx * nfeat
    for yy in range(NY):
        m = dot(down[:, yy * per_y : (yy + 1) * per_y], hidden, 0, 0).reshape(nz, nx, nfeat, ntok)
        mix[pl.ds(yy * nz, nz)] = m
        for xx in range(nx):
            mixa[yy * nx + xx] = m[:, xx, :fh].astype(BF16)
            mixb[:, yy * nx + xx] = m[:, xx, fh:].astype(BF16)
    for d in range(1, nz):
        zz, device = z_peer(d)
        start(mixb.at[zz], mrb.at[d], MB_Z, d, device)
    for d in range(1, nk):
        yy, xx, device = p_peer(d)
        start(mixa.at[yy * nx + xx], mra.at[d], MA_P, d, device)

    for d in range(1, groups):
        arrived(stats.at[d], STATS, d)
    sums = stat[...]
    for d in range(1, groups):
        sums += stats[d]
    pp, tt, pt = sums[0] + 1e-06, sums[1] + 1e-06, sums[2]
    inv = lax.rsqrt(pp * tt)
    kk, lane = iota((nk, cap_z), 0), iota((nk, cap_z), 1)
    ky = (y + NY - lax.shift_right_logical(kk, nx.bit_length() - 1)) & (NY - 1)
    kx = (x + nx - (kk & (nx - 1))) & (nx - 1)
    source = (ky * nz + lax.shift_right_logical(lane, 4)) * nx + kx
    valid = (source * CAP + (lane & (CAP - 1)) < counts[dp]).astype(F32)
    weight = valid * (ndp * nfeat / tokens)
    count = lax.fori_loop(0, ndp, lambda i, c: c + counts[i], jnp.int32(0))
    loss1[...] = valid * (1.0 - pt * inv)
    for d in range(1, nk):
        start(loss1, lossp.at[d], LOSS_P, d, p_peer(d)[2])
    a, b = weight * pt * inv / pp, weight * inv
    for k in range(nk):
        dpt[:, k * cap_z : (k + 1) * cap_z] = (
            a[k : k + 1] * pred[k] - b[k : k + 1] * tta[:, k].reshape(width, cap_z).astype(F32)
        ).astype(BF16)
    gw = dot(xt[...], dpt[...], 1, 1).reshape(nk, part, width)
    grad[...] = gw
    gs[...] = gw.astype(BF16)
    for d in range(1, nk):
        yy, xx, device = p_peer(d)
        start(gs.at[yy * nx + xx], gr.at[d], GRAD_P, d, device)

    m = mix[pl.ds(y * nz, nz), x, :fh]
    for d in range(1, nk):
        arrived(mra.at[d], MA_P, d)
        m += mra[d].astype(F32)
    mfa[...] = m
    m2a[...] = m.astype(BF16)
    for d in range(1, nz):
        zz, device = z_peer(d)
        start(m2a.at[zz], mr2a.at[d], MA_Z, d, device)
    for yy in range(NY):
        mfb[pl.ds(yy * nx, nx)] = mix[yy * nz + z, :, fh:]
    m = mfb[...]
    for d in range(1, nz):
        arrived(mrb.at[d], MB_Z, d)
        m += mrb[d].astype(F32)
    mfb[...] = m
    m2b[...] = m.astype(BF16)
    for d in range(1, nk):
        yy, xx, device = p_peer(d)
        start(m2b.at[yy * nx + xx], mr2b.at[d], MB_P, d, device)

    for d in range(1, nk):
        arrived(lossp.at[d], LOSS_P, d)
    part_loss = loss1[...]
    for d in range(1, nk):
        part_loss += lossp[d]
    loss2[...] = part_loss
    for d in range(1, nz):
        start(loss2, lossz.at[d], LOSS_Z, d, z_peer(d)[1])

    for d in range(1, nk):
        arrived(gr.at[d], GRAD_P, d)
    acc = grad[me]
    for d in range(1, nk):
        acc += gr[d].astype(F32)
    gacc[pl.ds(0, part)] = acc
    gacc[pl.ds(part, 16)] = jnp.zeros((16, width), F32)
    for zz in range(nz):
        piece = gacc[pl.ds(zz * out_rows, 16)]
        gzf[zz] = piece
        gz[zz] = piece.astype(BF16)
    for d in range(1, nz):
        zz, device = z_peer(d)
        start(gz.at[zz], gzr.at[d], GRAD_Z, d, device)

    m = xin[:fh] + mfa[z]
    for d in range(1, nz):
        arrived(mr2a.at[d], MA_Z, d)
        m += mr2a[d].astype(F32)
    tout[pl.ds(0, fh)] = m.astype(BF16)
    m = xin[fh:] + mfb[me]
    for d in range(1, nk):
        arrived(mr2b.at[d], MB_P, d)
        m += mr2b[d].astype(F32)
    tout[pl.ds(fh, fh)] = m.astype(BF16)

    for d in range(1, nz):
        arrived(lossz.at[d], LOSS_Z, d)
        part_loss += lossz[d]
    loss_out[0, 0] = jnp.sum(part_loss) / count.astype(F32)

    acc = gzf[z]
    for d in range(1, nz):
        arrived(gzr.at[d], GRAD_Z, d)
        acc += gzr[d].astype(F32)
    gout[...] = acc[:out_rows]

    for copy in started:
        copy.wait_send()


def on_device(
    nz, nx, teacher_in, norm_gain, gate_w, up_w, down_w, prev_rows, student_in, student_w, target_rows, counts
):
    nk = NY * nx
    ndp = nk * nz
    ntok, nfeat = teacher_in.shape
    trows, width = prev_rows.shape
    s_dev, ds = student_in.shape
    groups = lax.axis_size("grp")
    cap_z = nz * CAP
    part = ds // nk
    out_rows = part // nz
    d_model = ndp * nfeat
    vm = pl.BlockSpec(memory_space=pltpu.VMEM)
    hbm = pl.BlockSpec(memory_space=pl.ANY)
    sm = pl.BlockSpec(memory_space=pltpu.SMEM)
    v = pltpu.VMEM
    scratch = [
        v((2 * nfeat, d_model), BF16),
        v((nfeat, d_model), BF16),
        v((nk, nz, CAP, ds), BF16),
        v((ds, width), BF16),
        v((nk, CAP, ndp), jnp.int32),
        v((nz, nk, nfeat // 2, ntok), BF16),
        v((nk, nz, nfeat // 2, ntok), BF16),
        v((NY * nz, nx, nfeat, ntok), BF16),
        v((8, ntok), F32),
        v((8, ntok), F32),
        v((nz, 8, ntok), F32),
        v((nk, 8, ntok), F32),
        v((2, nz, trows, width // 2), BF16),
        v((nk, nz * trows, cap_z), BF16),
        v((2, nk, width // 2, cap_z), BF16),
        v((2, nk, width // 2, cap_z), BF16),
        v((width, ds), BF16),
        v((ds, s_dev), BF16),
        v((nk, width, cap_z), F32),
        v((3, nk, cap_z), F32),
        v((groups, 3, nk, cap_z), F32),
        v((width, s_dev), BF16),
        v((nk, part, width), F32),
        v((nk, part, width), BF16),
        v((nk, part, width), BF16),
        v((part + 16, width), F32),
        v((nz, 16, width), F32),
        v((nz, 16, width), BF16),
        v((nz, 16, width), BF16),
        v((nk, cap_z), F32),
        v((nk, cap_z), F32),
        v((nk, nk, cap_z), F32),
        v((nz, nk, cap_z), F32),
        v((NY * nz, nx, nfeat, ntok), F32),
        v((nk, nz, nfeat // 2, ntok), BF16),
        v((nz, nk, nfeat // 2, ntok), BF16),
        v((nk, nz, nfeat // 2, ntok), BF16),
        v((nz, nk, nfeat // 2, ntok), BF16),
        v((nz, nfeat // 2, ntok), F32),
        v((nk, nfeat // 2, ntok), F32),
        v((nz, nfeat // 2, ntok), BF16),
        v((nk, nfeat // 2, ntok), BF16),
        v((nz, nfeat // 2, ntok), BF16),
        v((nk, nfeat // 2, ntok), BF16),
        pltpu.SemaphoreType.DMA((STAGES, max(nk, nz, groups))),
        pltpu.SemaphoreType.DMA((STAGES, max(nk, nz, groups))),
        pltpu.SemaphoreType.DMA((NY + 4 + nk,)),
    ]
    tout, gout, loss = pl.pallas_call(
        functools.partial(kernel, nz, nx),
        out_shape=(
            jax.ShapeDtypeStruct((nfeat, ntok), BF16),
            jax.ShapeDtypeStruct((out_rows, width), F32),
            jax.ShapeDtypeStruct((1, 1), F32),
        ),
        in_specs=[vm, vm, vm, hbm, hbm, hbm, hbm, hbm, hbm, sm],
        out_specs=(vm, vm, sm),
        scratch_shapes=scratch,
        compiler_params=pltpu.CompilerParams(
            collective_id=0, has_side_effects=True, vmem_limit_bytes=60 * 1024 * 1024
        ),
        name="distill",
    )(
        teacher_in.T,
        norm_gain.reshape(1, nfeat),
        prev_rows,
        gate_w.T,
        up_w.T,
        down_w,
        student_in.reshape(NY, nz, nx, CAP, ds),
        student_w,
        target_rows.transpose(0, 2, 1).reshape(NY, nz, nx, CAP, ndp),
        counts,
    )
    return tout.T, gout, loss.reshape(())


def solution(mesh):
    in_specs = (
        P("grp", "dp"),
        P("dp"),
        P(None, "dp"),
        P(None, "dp"),
        P("dp", None),
        P("dp", "grp"),
        P("dp", None),
        P(None, "grp"),
        P(),
        P(),
    )
    out_specs = (P("grp", "dp"), P("dp", "grp"), P())
    nx = 4
    nz = mesh.shape["dp"] // (NY * nx)
    return jax.shard_map(
        functools.partial(on_device, nz, nx), mesh=mesh, in_specs=in_specs, out_specs=out_specs, check_vma=False
    )
```

```python
import functools

import jax
import jax.numpy as jnp
from jax import lax
from jax.experimental import pallas as pl
from jax.experimental.pallas import tpu as pltpu
from jax.sharding import PartitionSpec as P

NY = 2
CAP = 16
MESH = pl.DeviceIdType.MESH
F32 = jnp.float32
BF16 = jnp.bfloat16

(
    XA_P, XA_Z, XB_Z, XB_P, SS_Z, SS_P, ROWS_Z0, ROWS_Z1, ROWS_P0, ROWS_P1, STATS,
    MA_P, MA_Z, MB_Z, MB_P, GRAD_P, GRAD_Z, LOSS_P, LOSS_Z,
) = range(19)
STAGES = 19


def dot(a, b, ca, cb):
    return lax.dot_general(a, b, (((ca,), (cb,)), ((), ())), preferred_element_type=F32)


def iota(shape, axis):
    return lax.broadcasted_iota(jnp.int32, shape, axis)


def kernel(
    nz, nx,
    tin, gain, rows, gate_h, up_h, down_h, x_h, w_h, tr_h, counts,
    tout, gout, loss_out,
    gu, down, xv, wv, tr, xa, xb, xn, ss1, ss2, ssz, ssp, rz, hot, tts, tta, wt, xt, pred, stat, stats, dpt,
    grad, gs, gr, gacc, gzf, gz, gzr, loss1, loss2, lossp, lossz,
    mix, mixa, mixb, mra, mrb, mfa, mfb, m2a, m2b, mr2a, mr2b,
    send, recv, local,
):
    nk = NY * nx
    ndp = nk * nz
    groups = lax.axis_size("grp")
    g, dp = lax.axis_index("grp"), lax.axis_index("dp")
    y, z, x = dp // (nz * nx), (dp // nx) % nz, dp % nx
    me = y * nx + x
    nfeat, ntok = tin.shape
    trows, width = rows.shape
    ds = wv.shape[0]
    cap_z = nz * CAP
    tokens = cap_z * nk
    part = ds // nk
    out_rows = part // nz
    half, fh = width // 2, nfeat // 2

    def z_peer(d):
        zz = (z + d) % nz
        return zz, (g, (y * nz + zz) * nx + x)

    def p_peer(d):
        yy, xx = (y + d // nx) % NY, (x + d % nx) % nx
        return yy, xx, (g, (yy * nz + z) * nx + xx)

    def p_source(d):
        return (y + NY - d // nx) % NY, (x + nx - d % nx) % nx

    def g_peer(d):
        return ((g + d) % groups, dp)

    def rcopy(src, dst, stage, d, device):
        return pltpu.make_async_remote_copy(
            src_ref=src, dst_ref=dst, send_sem=send.at[stage, d], recv_sem=recv.at[stage, d],
            device_id=device, device_id_type=MESH,
        )

    started = []

    def start(*args):
        copy = rcopy(*args)
        copy.start()
        started.append(copy)

    def arrived(ref, stage, d):
        rcopy(ref, ref, stage, d, z_peer(1)[1]).wait_recv()

    loads = []

    def load(src, dst):
        copy = pltpu.make_async_copy(src, dst, local.at[len(loads)])
        copy.start()
        loads.append(copy)

    for yy in range(NY):
        load(tr_h.at[yy, z], tr.at[pl.ds(yy * nx, nx)])
    load(w_h, wv)
    for d in range(nk):
        yy, xx = p_source(d)
        load(x_h.at[yy, :, xx], xv.at[d])
    load(gate_h, gu.at[pl.ds(0, nfeat)])
    load(up_h, gu.at[pl.ds(nfeat, nfeat)])
    load(down_h, down)

    for c in range(2):
        rz[c, 0] = rows[:, c * half : (c + 1) * half]
    xin = tin[...].astype(F32)
    eye = iota((nfeat, nfeat), 0) == iota((nfeat, nfeat), 1)
    gain_col = jnp.sum(jnp.where(eye, gain[...].astype(F32), 0.0), axis=1, keepdims=True)
    xg = (xin * gain_col).astype(BF16)
    xa[0, 0] = xg[:fh]
    xb[0, 0] = xg[fh:]
    squares = jnp.sum((xin * xin).reshape(nfeat // 8, 8, ntok), axis=0)
    ss1[...] = squares

    barrier = pltpu.get_barrier_semaphore()
    peers = (
        [z_peer(d)[1] for d in range(1, nz)]
        + [p_peer(d)[2] for d in range(1, nk)]
        + [g_peer(d) for d in range(1, groups)]
    )
    for device in peers:
        pl.semaphore_signal(barrier, inc=1, device_id=device, device_id_type=MESH)
    pl.semaphore_wait(barrier, len(peers))

    for d in range(1, nz):
        start(xb.at[0, 0], xb.at[0, d], XB_Z, d, z_peer(d)[1])
        start(ss1, ssz.at[d], SS_Z, d, z_peer(d)[1])
    relay = nz == 8
    for c in range(2):
        for d in (2, 6, 1, 7) if relay else range(1, nz):
            start(rz.at[c, 0], rz.at[c, d], ROWS_Z0 + c, d, z_peer(d)[1])
    for d in range(1, nk):
        start(xa.at[0, 0], xa.at[0, d], XA_P, d, p_peer(d)[2])

    for copy in loads[:NY]:
        copy.wait()
    pick = (iota((ndp, cap_z), 0) == (y * nz + lax.shift_right_logical(iota((ndp, cap_z), 1), 4)) * nx + x)
    slots = dot(tr[...].reshape(nk * CAP, ndp).astype(F32).astype(BF16), pick.astype(F32).astype(BF16), 1, 0)
    mine = iota((nk, CAP, cap_z), 1) == (iota((nk, CAP, cap_z), 2) & (CAP - 1))
    target = jnp.sum(jnp.where(mine, slots.reshape(nk, CAP, cap_z), 0.0), axis=1)
    slot_z = (z + nz - lax.shift_right_logical(iota((nk, cap_z), 1), 4)) & (nz - 1)
    sel = target.astype(jnp.int32) + slot_z * trows
    row_of = iota((nz * trows, cap_z), 0)
    for k in range(nk):
        hot[k] = (row_of == sel[k : k + 1]).astype(F32).astype(BF16)

    for d in range(1, nz):
        arrived(xb.at[0, d], XB_Z, d)
        arrived(ssz.at[d], SS_Z, d)
        squares += ssz[d]
    ss2[...] = squares
    for d in range(1, nk):
        device = p_peer(d)[2]
        start(xb.at[0], xb.at[d], XB_P, d, device)
        start(ss2, ssp.at[d], SS_P, d, device)

    if relay:
        low, high = pl.ds(0, trows // 2), pl.ds(trows // 2, trows // 2)
        for c in range(2):
            stage = ROWS_Z0 + c
            arrived(rz.at[c, 2], stage, 2)
            start(rz.at[c, 2, low], rz.at[c, 4, low], stage, 4, z_peer(2)[1])
            start(rz.at[c, 2], rz.at[c, 3], stage, 3, z_peer(1)[1])
            arrived(rz.at[c, 6], stage, 6)
            start(rz.at[c, 6, high], rz.at[c, 4, high], stage, 0, z_peer(6)[1])
            start(rz.at[c, 6], rz.at[c, 5], stage, 5, z_peer(7)[1])

    for d in range(1, nk):
        arrived(xa.at[0, d], XA_P, d)
    for d in range(1, nz):
        start(xa.at[0], xa.at[d], XA_Z, d, z_peer(d)[1])

    for copy in loads[NY : NY + 1 + nk]:
        copy.wait()
    wt[...] = wv[...].T
    for k in range(nk):
        p = dot(wt[...], xv[k].reshape(cap_z, ds), 1, 1)
        pred[k] = p
        stat[0, k : k + 1, :] = jnp.sum(p * p, axis=0, keepdims=True)

    for c in range(2):
        stage = ROWS_Z0 + c
        if relay:
            for d in (1, 7, 3, 5):
                arrived(rz.at[c, d], stage, d)
            arrived(rz.at[c, 4, low], stage, 4)
            arrived(rz.at[c, 4, high], stage, 0)
        else:
            for d in range(1, nz):
                arrived(rz.at[c, d], stage, d)
        rz_t = rz[c].reshape(nz * trows, half).T
        for d in list(range(1, nk)) + [0]:
            yy, xx, device = p_peer(d)
            picked = dot(rz_t, hot[yy * nx + xx], 1, 0).astype(BF16)
            if d == 0:
                tta[c, 0] = picked
            else:
                tts[c, d] = picked
                start(tts.at[c, d], tta.at[c, d], ROWS_P0 + c, d, device)

    r = iota((ds, 1), 0).astype(F32)
    rk = jnp.floor((r + 0.5) / part)
    rz_ = jnp.floor((r - rk * part + 0.5) / out_rows)
    ry = jnp.floor((rk + 0.5) / nx)
    column = ((ry * nz + rz_) * nx + (rk - ry * nx)) * out_rows + (r - rk * part - rz_ * out_rows)
    order = (column == iota((ds, ds), 1).astype(F32)).astype(F32).astype(BF16)
    for k in range(nk):
        xt[:, k * cap_z : (k + 1) * cap_z] = dot(order, xv[k].reshape(cap_z, ds), 1, 1).astype(BF16)

    for d in range(nk):
        tt_sum = pt_sum = 0.0
        for c in range(2):
            if d:
                arrived(tta.at[c, d], ROWS_P0 + c, d)
            t = tta[c, d].astype(F32)
            tt_sum += jnp.sum(t * t, axis=0, keepdims=True)
            pt_sum += jnp.sum(t * pred[d, c * half : (c + 1) * half], axis=0, keepdims=True)
        stat[1, d : d + 1, :] = tt_sum
        stat[2, d : d + 1, :] = pt_sum
    for d in range(1, groups):
        start(stat, stats.at[d], STATS, d, g_peer(d))

    for d in range(1, nk):
        arrived(ssp.at[d], SS_P, d)
        squares += ssp[d]
        arrived(xb.at[d], XB_P, d)
    for d in range(1, nz):
        arrived(xa.at[d], XA_Z, d)
    total = jnp.sum(squares, axis=0, keepdims=True)
    scale = lax.rsqrt(total * (1.0 / (ndp * nfeat)) + 1e-05)
    for copy in loads[NY + 1 + nk :]:
        copy.wait()
    for d in range(nk):
        yy, xx = p_source(d)
        for dz in range(nz):
            place = yy * nz + (z + nz - dz) % nz
            xn[place, xx, :fh] = xa[dz, d]
            xn[place, xx, fh:] = xb[d, dz]
    h = dot(gu[...], xn[...].reshape(ndp * nfeat, ntok), 1, 0)
    gate, up = h[:nfeat] * scale, h[nfeat:] * scale
    hidden = (gate * jax.nn.sigmoid(gate) * up).astype(BF16)
    per_y = nz * nx * nfeat
    for yy in range(NY):
        m = dot(down[:, yy * per_y : (yy + 1) * per_y], hidden, 0, 0).reshape(nz, nx, nfeat, ntok)
        mix[pl.ds(yy * nz, nz)] = m
        for xx in range(nx):
            mixa[yy * nx + xx] = m[:, xx, :fh].astype(BF16)
            mixb[:, yy * nx + xx] = m[:, xx, fh:].astype(BF16)
    for d in range(1, nz):
        zz, device = z_peer(d)
        start(mixb.at[zz], mrb.at[d], MB_Z, d, device)
    for d in range(1, nk):
        yy, xx, device = p_peer(d)
        start(mixa.at[yy * nx + xx], mra.at[d], MA_P, d, device)

    for d in range(1, groups):
        arrived(stats.at[d], STATS, d)
    sums = stat[...]
    for d in range(1, groups):
        sums += stats[d]
    pp, tt, pt = sums[0] + 1e-06, sums[1] + 1e-06, sums[2]
    inv = lax.rsqrt(pp * tt)
    kk, lane = iota((nk, cap_z), 0), iota((nk, cap_z), 1)
    ky = (y + NY - lax.shift_right_logical(kk, nx.bit_length() - 1)) & (NY - 1)
    kx = (x + nx - (kk & (nx - 1))) & (nx - 1)
    source = (ky * nz + lax.shift_right_logical(lane, 4)) * nx + kx
    valid = (source * CAP + (lane & (CAP - 1)) < counts[dp]).astype(F32)
    weight = valid * (ndp * nfeat / tokens)
    count = lax.fori_loop(0, ndp, lambda i, c: c + counts[i], jnp.int32(0))
    loss1[...] = valid * (1.0 - pt * inv)
    for d in range(1, nk):
        start(loss1, lossp.at[d], LOSS_P, d, p_peer(d)[2])
    a, b = weight * pt * inv / pp, weight * inv
    for k in range(nk):
        dpt[:, k * cap_z : (k + 1) * cap_z] = (
            a[k : k + 1] * pred[k] - b[k : k + 1] * tta[:, k].reshape(width, cap_z).astype(F32)
        ).astype(BF16)
    gw = dot(xt[...], dpt[...], 1, 1).reshape(nk, part, width)
    grad[...] = gw
    gs[...] = gw.astype(BF16)
    for d in range(1, nk):
        yy, xx, device = p_peer(d)
        start(gs.at[yy * nx + xx], gr.at[d], GRAD_P, d, device)

    m = mix[pl.ds(y * nz, nz), x, :fh]
    for d in range(1, nk):
        arrived(mra.at[d], MA_P, d)
        m += mra[d].astype(F32)
    mfa[...] = m
    m2a[...] = m.astype(BF16)
    for d in range(1, nz):
        zz, device = z_peer(d)
        start(m2a.at[zz], mr2a.at[d], MA_Z, d, device)
    for yy in range(NY):
        mfb[pl.ds(yy * nx, nx)] = mix[yy * nz + z, :, fh:]
    m = mfb[...]
    for d in range(1, nz):
        arrived(mrb.at[d], MB_Z, d)
        m += mrb[d].astype(F32)
    mfb[...] = m
    m2b[...] = m.astype(BF16)
    for d in range(1, nk):
        yy, xx, device = p_peer(d)
        start(m2b.at[yy * nx + xx], mr2b.at[d], MB_P, d, device)

    for d in range(1, nk):
        arrived(lossp.at[d], LOSS_P, d)
    part_loss = loss1[...]
    for d in range(1, nk):
        part_loss += lossp[d]
    loss2[...] = part_loss
    for d in range(1, nz):
        start(loss2, lossz.at[d], LOSS_Z, d, z_peer(d)[1])

    for d in range(1, nk):
        arrived(gr.at[d], GRAD_P, d)
    acc = grad[me]
    for d in range(1, nk):
        acc += gr[d].astype(F32)
    gacc[pl.ds(0, part)] = acc
    gacc[pl.ds(part, 16)] = jnp.zeros((16, width), F32)
    for zz in range(nz):
        piece = gacc[pl.ds(zz * out_rows, 16)]
        gzf[zz] = piece
        gz[zz] = piece.astype(BF16)
    for d in range(1, nz):
        zz, device = z_peer(d)
        start(gz.at[zz], gzr.at[d], GRAD_Z, d, device)

    m = xin[:fh] + mfa[z]
    for d in range(1, nz):
        arrived(mr2a.at[d], MA_Z, d)
        m += mr2a[d].astype(F32)
    tout[pl.ds(0, fh)] = m.astype(BF16)
    m = xin[fh:] + mfb[me]
    for d in range(1, nk):
        arrived(mr2b.at[d], MB_P, d)
        m += mr2b[d].astype(F32)
    tout[pl.ds(fh, fh)] = m.astype(BF16)

    for d in range(1, nz):
        arrived(lossz.at[d], LOSS_Z, d)
        part_loss += lossz[d]
    loss_out[0, 0] = jnp.sum(part_loss) / count.astype(F32)

    acc = gzf[z]
    for d in range(1, nz):
        arrived(gzr.at[d], GRAD_Z, d)
        acc += gzr[d].astype(F32)
    gout[...] = acc[:out_rows]

    for copy in started:
        copy.wait_send()


def on_device(
    nz, nx, teacher_in, norm_gain, gate_w, up_w, down_w, prev_rows, student_in, student_w, target_rows, counts
):
    nk = NY * nx
    ndp = nk * nz
    ntok, nfeat = teacher_in.shape
    trows, width = prev_rows.shape
    s_dev, ds = student_in.shape
    groups = lax.axis_size("grp")
    cap_z = nz * CAP
    part = ds // nk
    out_rows = part // nz
    d_model = ndp * nfeat
    vm = pl.BlockSpec(memory_space=pltpu.VMEM)
    hbm = pl.BlockSpec(memory_space=pl.ANY)
    sm = pl.BlockSpec(memory_space=pltpu.SMEM)
    v = pltpu.VMEM
    scratch = [
        v((2 * nfeat, d_model), BF16),
        v((nfeat, d_model), BF16),
        v((nk, nz, CAP, ds), BF16),
        v((ds, width), BF16),
        v((nk, CAP, ndp), jnp.int32),
        v((nz, nk, nfeat // 2, ntok), BF16),
        v((nk, nz, nfeat // 2, ntok), BF16),
        v((NY * nz, nx, nfeat, ntok), BF16),
        v((8, ntok), F32),
        v((8, ntok), F32),
        v((nz, 8, ntok), F32),
        v((nk, 8, ntok), F32),
        v((2, nz, trows, width // 2), BF16),
        v((nk, nz * trows, cap_z), BF16),
        v((2, nk, width // 2, cap_z), BF16),
        v((2, nk, width // 2, cap_z), BF16),
        v((width, ds), BF16),
        v((ds, s_dev), BF16),
        v((nk, width, cap_z), F32),
        v((3, nk, cap_z), F32),
        v((groups, 3, nk, cap_z), F32),
        v((width, s_dev), BF16),
        v((nk, part, width), F32),
        v((nk, part, width), BF16),
        v((nk, part, width), BF16),
        v((part + 16, width), F32),
        v((nz, 16, width), F32),
        v((nz, 16, width), BF16),
        v((nz, 16, width), BF16),
        v((nk, cap_z), F32),
        v((nk, cap_z), F32),
        v((nk, nk, cap_z), F32),
        v((nz, nk, cap_z), F32),
        v((NY * nz, nx, nfeat, ntok), F32),
        v((nk, nz, nfeat // 2, ntok), BF16),
        v((nz, nk, nfeat // 2, ntok), BF16),
        v((nk, nz, nfeat // 2, ntok), BF16),
        v((nz, nk, nfeat // 2, ntok), BF16),
        v((nz, nfeat // 2, ntok), F32),
        v((nk, nfeat // 2, ntok), F32),
        v((nz, nfeat // 2, ntok), BF16),
        v((nk, nfeat // 2, ntok), BF16),
        v((nz, nfeat // 2, ntok), BF16),
        v((nk, nfeat // 2, ntok), BF16),
        pltpu.SemaphoreType.DMA((STAGES, max(nk, nz, groups))),
        pltpu.SemaphoreType.DMA((STAGES, max(nk, nz, groups))),
        pltpu.SemaphoreType.DMA((NY + 4 + nk,)),
    ]
    tout, gout, loss = pl.pallas_call(
        functools.partial(kernel, nz, nx),
        out_shape=(
            jax.ShapeDtypeStruct((nfeat, ntok), BF16),
            jax.ShapeDtypeStruct((out_rows, width), F32),
            jax.ShapeDtypeStruct((1, 1), F32),
        ),
        in_specs=[vm, vm, vm, hbm, hbm, hbm, hbm, hbm, hbm, sm],
        out_specs=(vm, vm, sm),
        scratch_shapes=scratch,
        compiler_params=pltpu.CompilerParams(
            collective_id=0, has_side_effects=True, vmem_limit_bytes=60 * 1024 * 1024
        ),
        name="distill",
    )(
        teacher_in.T,
        norm_gain.reshape(1, nfeat),
        prev_rows,
        gate_w.T,
        up_w.T,
        down_w,
        student_in.reshape(NY, nz, nx, CAP, ds),
        student_w,
        target_rows.transpose(0, 2, 1).reshape(NY, nz, nx, CAP, ndp),
        counts,
    )
    return tout.T, gout, loss.reshape(())


def solution(mesh):
    in_specs = (
        P("grp", "dp"),
        P("dp"),
        P(None, "dp"),
        P(None, "dp"),
        P("dp", None),
        P("dp", "grp"),
        P("dp", None),
        P(None, "grp"),
        P(),
        P(),
    )
    out_specs = (P("grp", "dp"), P("dp", "grp"), P())
    nx = 4
    nz = mesh.shape["dp"] // (NY * nx)
    return jax.shard_map(
        functools.partial(on_device, nz, nx), mesh=mesh, in_specs=in_specs, out_specs=out_specs, check_vma=False
    )
```

```python
import functools

import jax
import jax.numpy as jnp
from jax import lax
from jax.experimental import pallas as pl
from jax.experimental.pallas import tpu as pltpu
from jax.sharding import PartitionSpec as P

NY = 2
CAP = 16
FA = 32
MA = 48
MESH = pl.DeviceIdType.MESH
F32 = jnp.float32
BF16 = jnp.bfloat16

(
    XA_P, XA_Z, XB_Z, XB_P, SS_Z, SS_P, ROWS_Z0, ROWS_Z1, ROWS_P0, ROWS_P1, STATS,
    MA_P, MA_Z, MB_Z, MB_P, GA_P, GA_Z, GB_Z, GB_P, LOSS_P, LOSS_Z,
) = range(21)
STAGES = 21


def dot(a, b, ca, cb):
    return lax.dot_general(a, b, (((ca,), (cb,)), ((), ())), preferred_element_type=F32)


def iota(shape, axis):
    return lax.broadcasted_iota(jnp.int32, shape, axis)


def kernel(
    nz, nx,
    tin, gain, rows, gate_h, up_h, down_h, x_h, w_h, tr_h, counts,
    tout, gout, loss_out,
    gu, down, xv, wv, tr, xa, xb, xn, ss1, ss2, ssz, ssp, rz, hot, tts, tta, wt, xt, pred, stat, stats, dpt,
    grad, gs, gr, gacc, gz, gzr, gb, gbs, gbr, gb2, gbr2, loss1, loss2, lossp, lossz,
    mix, mixa, mixb, mra, mrb, mfa, mfb, m2a, m2b, mr2a, mr2b,
    send, recv, local,
):
    nk = NY * nx
    ndp = nk * nz
    groups = lax.axis_size("grp")
    g, dp = lax.axis_index("grp"), lax.axis_index("dp")
    y, z, x = dp // (nz * nx), (dp // nx) % nz, dp % nx
    me = y * nx + x
    nfeat, ntok = tin.shape
    trows, width = rows.shape
    ds = wv.shape[0]
    cap_z = nz * CAP
    tokens = cap_z * nk
    part = ds // nk
    out_rows = part // nz
    half = width // 2
    fa, ma = FA, MA
    wa = width - width // 4

    def z_peer(d):
        zz = (z + d) % nz
        return zz, (g, (y * nz + zz) * nx + x)

    def p_peer(d):
        yy, xx = (y + d // nx) % NY, (x + d % nx) % nx
        return yy, xx, (g, (yy * nz + z) * nx + xx)

    def p_source(d):
        return (y + NY - d // nx) % NY, (x + nx - d % nx) % nx

    def g_peer(d):
        return ((g + d) % groups, dp)

    def rcopy(src, dst, stage, d, device):
        return pltpu.make_async_remote_copy(
            src_ref=src, dst_ref=dst, send_sem=send.at[stage, d], recv_sem=recv.at[stage, d],
            device_id=device, device_id_type=MESH,
        )

    started = []

    def start(*args):
        copy = rcopy(*args)
        copy.start()
        started.append(copy)

    def arrived(ref, stage, d):
        rcopy(ref, ref, stage, d, z_peer(1)[1]).wait_recv()

    loads = []

    def load(src, dst):
        copy = pltpu.make_async_copy(src, dst, local.at[len(loads)])
        copy.start()
        loads.append(copy)

    for yy in range(NY):
        load(tr_h.at[yy, z], tr.at[pl.ds(yy * nx, nx)])
    load(w_h, wv)
    for d in range(nk):
        yy, xx = p_source(d)
        load(x_h.at[yy, :, xx], xv.at[d])
    load(gate_h, gu.at[pl.ds(0, nfeat)])
    load(up_h, gu.at[pl.ds(nfeat, nfeat)])
    load(down_h, down)

    for c in range(2):
        rz[c, 0] = rows[:, c * half : (c + 1) * half]
    xin = tin[...].astype(F32)
    eye = iota((nfeat, nfeat), 0) == iota((nfeat, nfeat), 1)
    gain_col = jnp.sum(jnp.where(eye, gain[...].astype(F32), 0.0), axis=1, keepdims=True)
    xg = (xin * gain_col).astype(BF16)
    xa[0, 0] = xg[:fa]
    xb[0, 0] = xg[fa:]
    squares = jnp.sum((xin * xin).reshape(nfeat // 8, 8, ntok), axis=0)
    ss1[...] = squares

    barrier = pltpu.get_barrier_semaphore()
    peers = (
        [z_peer(d)[1] for d in range(1, nz)]
        + [p_peer(d)[2] for d in range(1, nk)]
        + [g_peer(d) for d in range(1, groups)]
    )
    for device in peers:
        pl.semaphore_signal(barrier, inc=1, device_id=device, device_id_type=MESH)
    pl.semaphore_wait(barrier, len(peers))

    for d in range(1, nz):
        start(xb.at[0, 0], xb.at[0, d], XB_Z, d, z_peer(d)[1])
        start(ss1, ssz.at[d], SS_Z, d, z_peer(d)[1])
    relay = nz == 8
    for c in range(2):
        for d in (2, 6, 1, 7) if relay else range(1, nz):
            start(rz.at[c, 0], rz.at[c, d], ROWS_Z0 + c, d, z_peer(d)[1])
    for d in range(1, nk):
        start(xa.at[0, 0], xa.at[0, d], XA_P, d, p_peer(d)[2])

    for copy in loads[:NY]:
        copy.wait()
    pick = (iota((ndp, cap_z), 0) == (y * nz + lax.shift_right_logical(iota((ndp, cap_z), 1), 4)) * nx + x)
    slots = dot(tr[...].reshape(nk * CAP, ndp).astype(F32).astype(BF16), pick.astype(F32).astype(BF16), 1, 0)
    mine = iota((nk, CAP, cap_z), 1) == (iota((nk, CAP, cap_z), 2) & (CAP - 1))
    target = jnp.sum(jnp.where(mine, slots.reshape(nk, CAP, cap_z), 0.0), axis=1)
    slot_z = (z + nz - lax.shift_right_logical(iota((nk, cap_z), 1), 4)) & (nz - 1)
    sel = target.astype(jnp.int32) + slot_z * trows
    row_of = iota((nz * trows, cap_z), 0)
    for k in range(nk):
        hot[k] = (row_of == sel[k : k + 1]).astype(F32).astype(BF16)

    for d in range(1, nz):
        arrived(xb.at[0, d], XB_Z, d)
        arrived(ssz.at[d], SS_Z, d)
        squares += ssz[d]
    ss2[...] = squares
    for d in range(1, nk):
        device = p_peer(d)[2]
        start(xb.at[0], xb.at[d], XB_P, d, device)
        start(ss2, ssp.at[d], SS_P, d, device)

    if relay:
        low, high = pl.ds(0, trows // 2), pl.ds(trows // 2, trows // 2)
        for c in range(2):
            stage = ROWS_Z0 + c
            arrived(rz.at[c, 2], stage, 2)
            start(rz.at[c, 2, low], rz.at[c, 4, low], stage, 4, z_peer(2)[1])
            start(rz.at[c, 2], rz.at[c, 3], stage, 3, z_peer(1)[1])
            arrived(rz.at[c, 6], stage, 6)
            start(rz.at[c, 6, high], rz.at[c, 4, high], stage, 0, z_peer(6)[1])
            start(rz.at[c, 6], rz.at[c, 5], stage, 5, z_peer(7)[1])

    for d in range(1, nk):
        arrived(xa.at[0, d], XA_P, d)
    for d in range(1, nz):
        start(xa.at[0], xa.at[d], XA_Z, d, z_peer(d)[1])

    for copy in loads[NY : NY + 1 + nk]:
        copy.wait()
    wt[...] = wv[...].T
    for k in range(nk):
        p = dot(wt[...], xv[k].reshape(cap_z, ds), 1, 1)
        pred[k] = p
        stat[0, k : k + 1, :] = jnp.sum(p * p, axis=0, keepdims=True)

    for c in range(2):
        stage = ROWS_Z0 + c
        if relay:
            for d in (1, 7, 3, 5):
                arrived(rz.at[c, d], stage, d)
            arrived(rz.at[c, 4, low], stage, 4)
            arrived(rz.at[c, 4, high], stage, 0)
        else:
            for d in range(1, nz):
                arrived(rz.at[c, d], stage, d)
        rz_t = rz[c].reshape(nz * trows, half).T
        for d in list(range(1, nk)) + [0]:
            yy, xx, device = p_peer(d)
            picked = dot(rz_t, hot[yy * nx + xx], 1, 0).astype(BF16)
            if d == 0:
                tta[c, 0] = picked
            else:
                tts[c, d] = picked
                start(tts.at[c, d], tta.at[c, d], ROWS_P0 + c, d, device)

    r = iota((ds, 1), 0).astype(F32)
    rd = jnp.floor((r + 0.5) / part)
    rz_ = jnp.floor((r - rd * part + 0.5) / out_rows)
    ry = jnp.floor((rd + 0.5) / nx)

    def turn(v, n):
        return v - jnp.where(v > n - 0.5, float(n), 0.0)

    oy = turn(ry + y.astype(F32), NY)
    ox = turn(rd - ry * nx + x.astype(F32), nx)
    oz = turn(rz_ + z.astype(F32), nz)
    column = ((oy * nz + oz) * nx + ox) * out_rows + (r - rd * part - rz_ * out_rows)
    order = (column == iota((ds, ds), 1).astype(F32)).astype(F32).astype(BF16)
    for k in range(nk):
        xt[:, k * cap_z : (k + 1) * cap_z] = dot(order, xv[k].reshape(cap_z, ds), 1, 1).astype(BF16)

    for d in range(nk):
        tt_sum = pt_sum = 0.0
        for c in range(2):
            if d:
                arrived(tta.at[c, d], ROWS_P0 + c, d)
            t = tta[c, d].astype(F32)
            tt_sum += jnp.sum(t * t, axis=0, keepdims=True)
            pt_sum += jnp.sum(t * pred[d, c * half : (c + 1) * half], axis=0, keepdims=True)
        stat[1, d : d + 1, :] = tt_sum
        stat[2, d : d + 1, :] = pt_sum
    for d in range(1, groups):
        start(stat, stats.at[d], STATS, d, g_peer(d))

    for d in range(1, nk):
        arrived(ssp.at[d], SS_P, d)
        squares += ssp[d]
        arrived(xb.at[d], XB_P, d)
    for d in range(1, nz):
        arrived(xa.at[d], XA_Z, d)
    total = jnp.sum(squares, axis=0, keepdims=True)
    scale = lax.rsqrt(total * (1.0 / (ndp * nfeat)) + 1e-05)
    for copy in loads[NY + 1 + nk :]:
        copy.wait()
    for d in range(nk):
        yy, xx = p_source(d)
        for dz in range(nz):
            place = yy * nz + (z + nz - dz) % nz
            xn[place, xx, :fa] = xa[dz, d]
            xn[place, xx, fa:] = xb[d, dz]
    h = dot(gu[...], xn[...].reshape(ndp * nfeat, ntok), 1, 0)
    gate, up = h[:nfeat] * scale, h[nfeat:] * scale
    hidden = (gate * jax.nn.sigmoid(gate) * up).astype(BF16)
    per_y = nz * nx * nfeat
    for yy in range(NY):
        m = dot(down[:, yy * per_y : (yy + 1) * per_y], hidden, 0, 0).reshape(nz, nx, nfeat, ntok)
        mix[pl.ds(yy * nz, nz)] = m
        for xx in range(nx):
            mixa[yy * nx + xx] = m[:, xx, :ma].astype(BF16)
            mixb[:, yy * nx + xx] = m[:, xx, ma:].astype(BF16)
    for d in range(1, nz):
        zz, device = z_peer(d)
        start(mixb.at[zz], mrb.at[d], MB_Z, d, device)
    for d in range(1, nk):
        yy, xx, device = p_peer(d)
        start(mixa.at[yy * nx + xx], mra.at[d], MA_P, d, device)

    for d in range(1, groups):
        arrived(stats.at[d], STATS, d)
    sums = stat[...]
    for d in range(1, groups):
        sums += stats[d]
    pp, tt, pt = sums[0] + 1e-06, sums[1] + 1e-06, sums[2]
    inv = lax.rsqrt(pp * tt)
    kk, lane = iota((nk, cap_z), 0), iota((nk, cap_z), 1)
    ky = (y + NY - lax.shift_right_logical(kk, nx.bit_length() - 1)) & (NY - 1)
    kx = (x + nx - (kk & (nx - 1))) & (nx - 1)
    source = (ky * nz + lax.shift_right_logical(lane, 4)) * nx + kx
    valid = (source * CAP + (lane & (CAP - 1)) < counts[dp]).astype(F32)
    weight = valid * (ndp * nfeat / tokens)
    count = lax.fori_loop(0, ndp, lambda i, c: c + counts[i], jnp.int32(0))
    loss1[...] = valid * (1.0 - pt * inv)
    for d in range(1, nk):
        start(loss1, lossp.at[d], LOSS_P, d, p_peer(d)[2])
    a, b = weight * pt * inv / pp, weight * inv
    for k in range(nk):
        dpt[:, k * cap_z : (k + 1) * cap_z] = (
            a[k : k + 1] * pred[k] - b[k : k + 1] * tta[:, k].reshape(width, cap_z).astype(F32)
        ).astype(BF16)
    for first in range(0, nk, nk // 2):
        many = nk // 2 * part
        gw = dot(xt[first * part : first * part + many], dpt[...], 1, 1)
        gb[first * part : first * part + many] = gw[:, wa:]
        for d in range(first, first + nk // 2):
            piece = gw[(d - first) * part : (d - first + 1) * part, :wa]
            if d == 0:
                grad[...] = piece
            else:
                gs[d] = piece.astype(BF16)
                start(gs.at[d], gr.at[d], GA_P, d, p_peer(d)[2])
    gb[pl.ds(ds, 16)] = jnp.zeros((16, width - wa), F32)
    for dz in range(1, nz):
        for d in range(nk):
            gbs[dz, d] = gb[pl.ds(d * part + dz * out_rows, 16)].astype(BF16)
        start(gbs.at[dz], gbr.at[dz], GB_Z, dz, z_peer(dz)[1])

    m = mix[pl.ds(y * nz, nz), x, :ma]
    for d in range(1, nk):
        arrived(mra.at[d], MA_P, d)
        m += mra[d].astype(F32)
    mfa[...] = m
    m2a[...] = m.astype(BF16)
    for d in range(1, nz):
        zz, device = z_peer(d)
        start(m2a.at[zz], mr2a.at[d], MA_Z, d, device)
    acc = grad[...]
    for d in range(1, nk):
        arrived(gr.at[d], GA_P, d)
        acc += gr[d].astype(F32)
    gacc[pl.ds(0, part)] = acc
    gacc[pl.ds(part, 16)] = jnp.zeros((16, wa), F32)
    for dz in range(1, nz):
        gz[dz] = gacc[pl.ds(dz * out_rows, 16)].astype(BF16)
        start(gz.at[dz], gzr.at[dz], GA_Z, dz, z_peer(dz)[1])

    for yy in range(NY):
        mfb[pl.ds(yy * nx, nx)] = mix[yy * nz + z, :, ma:]
    m = mfb[...]
    for d in range(1, nz):
        arrived(mrb.at[d], MB_Z, d)
        m += mrb[d].astype(F32)
    mfb[...] = m
    m2b[...] = m.astype(BF16)
    for d in range(1, nk):
        yy, xx, device = p_peer(d)
        start(m2b.at[yy * nx + xx], mr2b.at[d], MB_P, d, device)

    sums_b = [gb[pl.ds(d * part, 16)] for d in range(nk)]
    for dz in range(1, nz):
        arrived(gbr.at[dz], GB_Z, dz)
        for d in range(nk):
            sums_b[d] += gbr[dz, d].astype(F32)
    for d in range(1, nk):
        gb2[d] = sums_b[d].astype(BF16)
        start(gb2.at[d], gbr2.at[d], GB_P, d, p_peer(d)[2])

    for d in range(1, nk):
        arrived(lossp.at[d], LOSS_P, d)
    part_loss = loss1[...]
    for d in range(1, nk):
        part_loss += lossp[d]
    loss2[...] = part_loss
    for d in range(1, nz):
        start(loss2, lossz.at[d], LOSS_Z, d, z_peer(d)[1])

    m = xin[:ma] + mfa[z]
    for d in range(1, nz):
        arrived(mr2a.at[d], MA_Z, d)
        m += mr2a[d].astype(F32)
    tout[pl.ds(0, ma)] = m.astype(BF16)
    m = xin[ma:] + mfb[me]
    for d in range(1, nk):
        arrived(mr2b.at[d], MB_P, d)
        m += mr2b[d].astype(F32)
    tout[pl.ds(ma, nfeat - ma)] = m.astype(BF16)

    for d in range(1, nz):
        arrived(lossz.at[d], LOSS_Z, d)
        part_loss += lossz[d]
    loss_out[0, 0] = jnp.sum(part_loss) / count.astype(F32)

    acc = gacc[pl.ds(0, 16)]
    for dz in range(1, nz):
        arrived(gzr.at[dz], GA_Z, dz)
        acc += gzr[dz].astype(F32)
    gout[:, :wa] = acc[:out_rows]
    acc = sums_b[0]
    for d in range(1, nk):
        arrived(gbr2.at[d], GB_P, d)
        acc += gbr2[d].astype(F32)
    gout[:, wa:] = acc[:out_rows]

    for copy in started:
        copy.wait_send()


def on_device(
    nz, nx, teacher_in, norm_gain, gate_w, up_w, down_w, prev_rows, student_in, student_w, target_rows, counts
):
    nk = NY * nx
    ndp = nk * nz
    ntok, nfeat = teacher_in.shape
    trows, width = prev_rows.shape
    s_dev, ds = student_in.shape
    groups = lax.axis_size("grp")
    cap_z = nz * CAP
    part = ds // nk
    out_rows = part // nz
    d_model = ndp * nfeat
    wa = width - width // 4
    vm = pl.BlockSpec(memory_space=pltpu.VMEM)
    hbm = pl.BlockSpec(memory_space=pl.ANY)
    sm = pl.BlockSpec(memory_space=pltpu.SMEM)
    v = pltpu.VMEM
    scratch = [
        v((2 * nfeat, d_model), BF16),
        v((nfeat, d_model), BF16),
        v((nk, nz, CAP, ds), BF16),
        v((ds, width), BF16),
        v((nk, CAP, ndp), jnp.int32),
        v((nz, nk, FA, ntok), BF16),
        v((nk, nz, nfeat - FA, ntok), BF16),
        v((NY * nz, nx, nfeat, ntok), BF16),
        v((8, ntok), F32),
        v((8, ntok), F32),
        v((nz, 8, ntok), F32),
        v((nk, 8, ntok), F32),
        v((2, nz, trows, width // 2), BF16),
        v((nk, nz * trows, cap_z), BF16),
        v((2, nk, width // 2, cap_z), BF16),
        v((2, nk, width // 2, cap_z), BF16),
        v((width, ds), BF16),
        v((ds, s_dev), BF16),
        v((nk, width, cap_z), F32),
        v((3, nk, cap_z), F32),
        v((groups, 3, nk, cap_z), F32),
        v((width, s_dev), BF16),
        v((part, wa), F32),
        v((nk, part, wa), BF16),
        v((nk, part, wa), BF16),
        v((part + 16, wa), F32),
        v((nz, 16, wa), BF16),
        v((nz, 16, wa), BF16),
        v((ds + 16, width - wa), F32),
        v((nz, nk, 16, width - wa), BF16),
        v((nz, nk, 16, width - wa), BF16),
        v((nk, 16, width - wa), BF16),
        v((nk, 16, width - wa), BF16),
        v((nk, cap_z), F32),
        v((nk, cap_z), F32),
        v((nk, nk, cap_z), F32),
        v((nz, nk, cap_z), F32),
        v((NY * nz, nx, nfeat, ntok), F32),
        v((nk, nz, MA, ntok), BF16),
        v((nz, nk, nfeat - MA, ntok), BF16),
        v((nk, nz, MA, ntok), BF16),
        v((nz, nk, nfeat - MA, ntok), BF16),
        v((nz, MA, ntok), F32),
        v((nk, nfeat - MA, ntok), F32),
        v((nz, MA, ntok), BF16),
        v((nk, nfeat - MA, ntok), BF16),
        v((nz, MA, ntok), BF16),
        v((nk, nfeat - MA, ntok), BF16),
        pltpu.SemaphoreType.DMA((STAGES, max(nk, nz, groups))),
        pltpu.SemaphoreType.DMA((STAGES, max(nk, nz, groups))),
        pltpu.SemaphoreType.DMA((NY + 4 + nk,)),
    ]
    tout, gout, loss = pl.pallas_call(
        functools.partial(kernel, nz, nx),
        out_shape=(
            jax.ShapeDtypeStruct((nfeat, ntok), BF16),
            jax.ShapeDtypeStruct((out_rows, width), F32),
            jax.ShapeDtypeStruct((1, 1), F32),
        ),
        in_specs=[vm, vm, vm, hbm, hbm, hbm, hbm, hbm, hbm, sm],
        out_specs=(vm, vm, sm),
        scratch_shapes=scratch,
        compiler_params=pltpu.CompilerParams(
            collective_id=0, has_side_effects=True, vmem_limit_bytes=60 * 1024 * 1024
        ),
        name="distill",
    )(
        teacher_in.T,
        norm_gain.reshape(1, nfeat),
        prev_rows,
        gate_w.T,
        up_w.T,
        down_w,
        student_in.reshape(NY, nz, nx, CAP, ds),
        student_w,
        target_rows.transpose(0, 2, 1).reshape(NY, nz, nx, CAP, ndp),
        counts,
    )
    return tout.T, gout, loss.reshape(())


def solution(mesh):
    in_specs = (
        P("grp", "dp"),
        P("dp"),
        P(None, "dp"),
        P(None, "dp"),
        P("dp", None),
        P("dp", "grp"),
        P("dp", None),
        P(None, "grp"),
        P(),
        P(),
    )
    out_specs = (P("grp", "dp"), P("dp", "grp"), P())
    nx = 4
    nz = mesh.shape["dp"] // (NY * nx)
    return jax.shard_map(
        functools.partial(on_device, nz, nx), mesh=mesh, in_specs=in_specs, out_specs=out_specs, check_vma=False
    )
```

```python
import functools

import jax
import jax.numpy as jnp
from jax import lax
from jax.experimental import pallas as pl
from jax.experimental.pallas import tpu as pltpu
from jax.sharding import PartitionSpec as P

NY = 2
CAP = 16
FA = 32
MA = 48
MESH = pl.DeviceIdType.MESH
F32 = jnp.float32
BF16 = jnp.bfloat16

(
    XA_P, XA_Z, XB_Z, XB_P, SS_Z, SS_P, ROWS_Z0, ROWS_Z1, ROWS_P0, ROWS_P1, STATS,
    MA_P, MA_Z, MB_Z, MB_P, GA_P, GA_Z, GB_Z, GB_P, LOSS_P, LOSS_Z,
) = range(21)
STAGES = 21


def dot(a, b, ca, cb):
    return lax.dot_general(a, b, (((ca,), (cb,)), ((), ())), preferred_element_type=F32)


def iota(shape, axis):
    return lax.broadcasted_iota(jnp.int32, shape, axis)


def kernel(
    nz, nx,
    tin, gain, rows, gate_h, up_h, down_h, x_h, w_h, tr_h, counts,
    tout, gout, loss_out,
    gu, down, xv, wv, tr, xa, xb, xn, ss1, ss2, ssz, ssp, rz, hot, tts, tta, wt, xt, pred, stat, stats, dpt,
    grad, gs, gr, gacc, gz, gzr, gb, gbs, gbr, gb2, gbr2, loss1, loss2, lossp, lossz,
    mix, mixa, mixb, mra, mrb, mfa, mfb, m2a, m2b, mr2a, mr2b,
    send, recv, local,
):
    nk = NY * nx
    ndp = nk * nz
    groups = lax.axis_size("grp")
    g, dp = lax.axis_index("grp"), lax.axis_index("dp")
    y, z, x = dp // (nz * nx), (dp // nx) % nz, dp % nx
    me = y * nx + x
    nfeat, ntok = tin.shape
    trows, width = rows.shape
    ds = wv.shape[0]
    cap_z = nz * CAP
    tokens = cap_z * nk
    part = ds // nk
    out_rows = part // nz
    half = width // 2
    fa, ma = FA, MA
    wa = width - width // 4

    def z_peer(d):
        zz = (z + d) % nz
        return zz, (g, (y * nz + zz) * nx + x)

    def p_peer(d):
        yy, xx = (y + d // nx) % NY, (x + d % nx) % nx
        return yy, xx, (g, (yy * nz + z) * nx + xx)

    def p_source(d):
        return (y + NY - d // nx) % NY, (x + nx - d % nx) % nx

    def g_peer(d):
        return ((g + d) % groups, dp)

    def rcopy(src, dst, stage, d, device):
        return pltpu.make_async_remote_copy(
            src_ref=src, dst_ref=dst, send_sem=send.at[stage, d], recv_sem=recv.at[stage, d],
            device_id=device, device_id_type=MESH,
        )

    started = []

    def start(*args):
        copy = rcopy(*args)
        copy.start()
        started.append(copy)

    def arrived(ref, stage, d):
        rcopy(ref, ref, stage, d, z_peer(1)[1]).wait_recv()

    loads = []

    def load(src, dst):
        copy = pltpu.make_async_copy(src, dst, local.at[len(loads)])
        copy.start()
        loads.append(copy)

    for yy in range(NY):
        load(tr_h.at[yy, z], tr.at[pl.ds(yy * nx, nx)])
    load(w_h, wv)
    for d in range(nk):
        yy, xx = p_source(d)
        load(x_h.at[yy, :, xx], xv.at[d])
    load(gate_h, gu.at[pl.ds(0, nfeat)])
    load(up_h, gu.at[pl.ds(nfeat, nfeat)])
    load(down_h, down)

    for c in range(2):
        rz[c, 0] = rows[:, c * half : (c + 1) * half]
    xin = tin[...].astype(F32)
    eye = iota((nfeat, nfeat), 0) == iota((nfeat, nfeat), 1)
    gain_col = jnp.sum(jnp.where(eye, gain[...].astype(F32), 0.0), axis=1, keepdims=True)
    xg = (xin * gain_col).astype(BF16)
    xa[0, 0] = xg[:fa]
    xb[0, 0] = xg[fa:]
    squares = jnp.sum((xin * xin).reshape(nfeat // 8, 8, ntok), axis=0)
    ss1[...] = squares

    barrier = pltpu.get_barrier_semaphore()
    peers = (
        [z_peer(d)[1] for d in range(1, nz)]
        + [p_peer(d)[2] for d in range(1, nk)]
        + [g_peer(d) for d in range(1, groups)]
    )
    for device in peers:
        pl.semaphore_signal(barrier, inc=1, device_id=device, device_id_type=MESH)
    pl.semaphore_wait(barrier, len(peers))

    for d in range(1, nz):
        start(xb.at[0, 0], xb.at[0, d], XB_Z, d, z_peer(d)[1])
        start(ss1, ssz.at[d], SS_Z, d, z_peer(d)[1])
    relay = nz == 8
    for c in range(2):
        for d in (2, 6, 1, 7) if relay else range(1, nz):
            start(rz.at[c, 0], rz.at[c, d], ROWS_Z0 + c, d, z_peer(d)[1])
    for d in range(1, nk):
        start(xa.at[0, 0], xa.at[0, d], XA_P, d, p_peer(d)[2])

    for copy in loads[:NY]:
        copy.wait()
    pick = (iota((ndp, cap_z), 0) == (y * nz + lax.shift_right_logical(iota((ndp, cap_z), 1), 4)) * nx + x)
    slots = dot(tr[...].reshape(nk * CAP, ndp).astype(F32).astype(BF16), pick.astype(F32).astype(BF16), 1, 0)
    mine = iota((nk, CAP, cap_z), 1) == (iota((nk, CAP, cap_z), 2) & (CAP - 1))
    target = jnp.sum(jnp.where(mine, slots.reshape(nk, CAP, cap_z), 0.0), axis=1)
    slot_z = (z + nz - lax.shift_right_logical(iota((nk, cap_z), 1), 4)) & (nz - 1)
    sel = target.astype(jnp.int32) + slot_z * trows
    row_of = iota((nz * trows, cap_z), 0)
    for k in range(nk):
        hot[k] = (row_of == sel[k : k + 1]).astype(F32).astype(BF16)

    for d in range(1, nz):
        arrived(xb.at[0, d], XB_Z, d)
        arrived(ssz.at[d], SS_Z, d)
        squares += ssz[d]
    ss2[...] = squares
    for d in range(1, nk):
        device = p_peer(d)[2]
        start(xb.at[0], xb.at[d], XB_P, d, device)
        start(ss2, ssp.at[d], SS_P, d, device)

    if relay:
        low, high = pl.ds(0, trows // 2), pl.ds(trows // 2, trows // 2)
        for c in range(2):
            stage = ROWS_Z0 + c
            arrived(rz.at[c, 2], stage, 2)
            start(rz.at[c, 2, low], rz.at[c, 4, low], stage, 4, z_peer(2)[1])
            start(rz.at[c, 2], rz.at[c, 3], stage, 3, z_peer(1)[1])
            arrived(rz.at[c, 6], stage, 6)
            start(rz.at[c, 6, high], rz.at[c, 4, high], stage, 0, z_peer(6)[1])
            start(rz.at[c, 6], rz.at[c, 5], stage, 5, z_peer(7)[1])

    for d in range(1, nk):
        arrived(xa.at[0, d], XA_P, d)
    for d in range(1, nz):
        start(xa.at[0], xa.at[d], XA_Z, d, z_peer(d)[1])

    for copy in loads[NY : NY + 1 + nk]:
        copy.wait()
    wt[...] = wv[...].T
    for k in range(nk):
        p = dot(wt[...], xv[k].reshape(cap_z, ds), 1, 1)
        pred[k] = p
        stat[0, k : k + 1, :] = jnp.sum(p * p, axis=0, keepdims=True)

    for c in range(2):
        stage = ROWS_Z0 + c
        if relay:
            for d in (1, 7, 3, 5):
                arrived(rz.at[c, d], stage, d)
            arrived(rz.at[c, 4, low], stage, 4)
            arrived(rz.at[c, 4, high], stage, 0)
        else:
            for d in range(1, nz):
                arrived(rz.at[c, d], stage, d)
        rz_t = rz[c].reshape(nz * trows, half).T
        for d in list(range(1, nk)) + [0]:
            yy, xx, device = p_peer(d)
            picked = dot(rz_t, hot[yy * nx + xx], 1, 0).astype(BF16)
            if d == 0:
                tta[c, 0] = picked
            else:
                tts[c, d] = picked
                start(tts.at[c, d], tta.at[c, d], ROWS_P0 + c, d, device)

    r = iota((ds, 1), 0).astype(F32)
    rd = jnp.floor((r + 0.5) / part)
    rz_ = jnp.floor((r - rd * part + 0.5) / out_rows)
    ry = jnp.floor((rd + 0.5) / nx)

    def turn(v, n):
        return v - jnp.where(v > n - 0.5, float(n), 0.0)

    oy = turn(ry + y.astype(F32), NY)
    ox = turn(rd - ry * nx + x.astype(F32), nx)
    oz = turn(rz_ + z.astype(F32), nz)
    column = ((oy * nz + oz) * nx + ox) * out_rows + (r - rd * part - rz_ * out_rows)
    order = (column == iota((ds, ds), 1).astype(F32)).astype(F32).astype(BF16)
    for k in range(nk):
        xt[:, k * cap_z : (k + 1) * cap_z] = dot(order, xv[k].reshape(cap_z, ds), 1, 1).astype(BF16)

    for d in range(nk):
        tt_sum = pt_sum = 0.0
        for c in range(2):
            if d:
                arrived(tta.at[c, d], ROWS_P0 + c, d)
            t = tta[c, d].astype(F32)
            tt_sum += jnp.sum(t * t, axis=0, keepdims=True)
            pt_sum += jnp.sum(t * pred[d, c * half : (c + 1) * half], axis=0, keepdims=True)
        stat[1, d : d + 1, :] = tt_sum
        stat[2, d : d + 1, :] = pt_sum
    for d in range(1, groups):
        start(stat, stats.at[d], STATS, d, g_peer(d))

    for d in range(1, nk):
        arrived(ssp.at[d], SS_P, d)
        squares += ssp[d]
        arrived(xb.at[d], XB_P, d)
    for d in range(1, nz):
        arrived(xa.at[d], XA_Z, d)
    total = jnp.sum(squares, axis=0, keepdims=True)
    scale = lax.rsqrt(total * (1.0 / (ndp * nfeat)) + 1e-05)
    for copy in loads[NY + 1 + nk :]:
        copy.wait()
    for d in range(nk):
        yy, xx = p_source(d)
        for dz in range(nz):
            place = yy * nz + (z + nz - dz) % nz
            xn[place, xx, :fa] = xa[dz, d]
            xn[place, xx, fa:] = xb[d, dz]
    h = dot(gu[...], xn[...].reshape(ndp * nfeat, ntok), 1, 0)
    gate, up = h[:nfeat] * scale, h[nfeat:] * scale
    hidden = (gate * jax.nn.sigmoid(gate) * up).astype(BF16)
    per_y = nz * nx * nfeat
    for yy in range(NY):
        m = dot(down[:, yy * per_y : (yy + 1) * per_y], hidden, 0, 0).reshape(nz, nx, nfeat, ntok)
        mix[pl.ds(yy * nz, nz)] = m
        for xx in range(nx):
            mixa[yy * nx + xx] = m[:, xx, :ma].astype(BF16)
            mixb[:, yy * nx + xx] = m[:, xx, ma:].astype(BF16)
    for d in range(1, nk):
        yy, xx, device = p_peer(d)
        start(mixa.at[yy * nx + xx], mra.at[d], MA_P, d, device)
    for d in range(1, nz):
        zz, device = z_peer(d)
        start(mixb.at[zz], mrb.at[d], MB_Z, d, device)

    for d in range(1, groups):
        arrived(stats.at[d], STATS, d)
    sums = stat[...]
    for d in range(1, groups):
        sums += stats[d]
    pp, tt, pt = sums[0] + 1e-06, sums[1] + 1e-06, sums[2]
    inv = lax.rsqrt(pp * tt)
    kk, lane = iota((nk, cap_z), 0), iota((nk, cap_z), 1)
    ky = (y + NY - lax.shift_right_logical(kk, nx.bit_length() - 1)) & (NY - 1)
    kx = (x + nx - (kk & (nx - 1))) & (nx - 1)
    source = (ky * nz + lax.shift_right_logical(lane, 4)) * nx + kx
    valid = (source * CAP + (lane & (CAP - 1)) < counts[dp]).astype(F32)
    weight = valid * (ndp * nfeat / tokens)
    count = lax.fori_loop(0, ndp, lambda i, c: c + counts[i], jnp.int32(0))
    loss1[...] = valid * (1.0 - pt * inv)
    for d in range(1, nk):
        start(loss1, lossp.at[d], LOSS_P, d, p_peer(d)[2])
    a, b = weight * pt * inv / pp, weight * inv
    for k in range(nk):
        dpt[:, k * cap_z : (k + 1) * cap_z] = (
            a[k : k + 1] * pred[k] - b[k : k + 1] * tta[:, k].reshape(width, cap_z).astype(F32)
        ).astype(BF16)
    for first in range(0, nk, nk // 2):
        many = nk // 2 * part
        gw = dot(xt[first * part : first * part + many], dpt[...], 1, 1)
        gb[first * part : first * part + many] = gw[:, wa:]
        for d in range(first, first + nk // 2):
            piece = gw[(d - first) * part : (d - first + 1) * part, :wa]
            if d == 0:
                grad[...] = piece
            else:
                gs[d] = piece.astype(BF16)
                start(gs.at[d], gr.at[d], GA_P, d, p_peer(d)[2])
    gb[pl.ds(ds, 16)] = jnp.zeros((16, width - wa), F32)
    for dz in range(1, nz):
        for d in range(nk):
            gbs[dz, d] = gb[pl.ds(d * part + dz * out_rows, 16)].astype(BF16)
        start(gbs.at[dz], gbr.at[dz], GB_Z, dz, z_peer(dz)[1])

    m = mix[pl.ds(y * nz, nz), x, :ma]
    for d in range(1, nk):
        arrived(mra.at[d], MA_P, d)
        m += mra[d].astype(F32)
    mfa[...] = m
    m2a[...] = m.astype(BF16)
    for d in range(1, nz):
        zz, device = z_peer(d)
        start(m2a.at[zz], mr2a.at[d], MA_Z, d, device)
    acc = grad[...]
    for d in range(1, nk):
        arrived(gr.at[d], GA_P, d)
        acc += gr[d].astype(F32)
    gacc[pl.ds(0, part)] = acc
    gacc[pl.ds(part, 16)] = jnp.zeros((16, wa), F32)
    for dz in range(1, nz):
        gz[dz] = gacc[pl.ds(dz * out_rows, 16)].astype(BF16)
        start(gz.at[dz], gzr.at[dz], GA_Z, dz, z_peer(dz)[1])

    for yy in range(NY):
        mfb[pl.ds(yy * nx, nx)] = mix[yy * nz + z, :, ma:]
    m = mfb[...]
    for d in range(1, nz):
        arrived(mrb.at[d], MB_Z, d)
        m += mrb[d].astype(F32)
    mfb[...] = m
    m2b[...] = m.astype(BF16)
    for d in range(1, nk):
        yy, xx, device = p_peer(d)
        start(m2b.at[yy * nx + xx], mr2b.at[d], MB_P, d, device)

    sums_b = [gb[pl.ds(d * part, 16)] for d in range(nk)]
    for dz in range(1, nz):
        arrived(gbr.at[dz], GB_Z, dz)
        for d in range(nk):
            sums_b[d] += gbr[dz, d].astype(F32)
    for d in range(1, nk):
        gb2[d] = sums_b[d].astype(BF16)
        start(gb2.at[d], gbr2.at[d], GB_P, d, p_peer(d)[2])

    for d in range(1, nk):
        arrived(lossp.at[d], LOSS_P, d)
    part_loss = loss1[...]
    for d in range(1, nk):
        part_loss += lossp[d]
    loss2[...] = part_loss
    for d in range(1, nz):
        start(loss2, lossz.at[d], LOSS_Z, d, z_peer(d)[1])

    m = xin[:ma] + mfa[z]
    for d in range(1, nz):
        arrived(mr2a.at[d], MA_Z, d)
        m += mr2a[d].astype(F32)
    tout[pl.ds(0, ma)] = m.astype(BF16)
    m = xin[ma:] + mfb[me]
    for d in range(1, nk):
        arrived(mr2b.at[d], MB_P, d)
        m += mr2b[d].astype(F32)
    tout[pl.ds(ma, nfeat - ma)] = m.astype(BF16)

    for d in range(1, nz):
        arrived(lossz.at[d], LOSS_Z, d)
        part_loss += lossz[d]
    loss_out[0, 0] = jnp.sum(part_loss) / count.astype(F32)

    acc = gacc[pl.ds(0, 16)]
    for dz in range(1, nz):
        arrived(gzr.at[dz], GA_Z, dz)
        acc += gzr[dz].astype(F32)
    gout[:, :wa] = acc[:out_rows]
    acc = sums_b[0]
    for d in range(1, nk):
        arrived(gbr2.at[d], GB_P, d)
        acc += gbr2[d].astype(F32)
    gout[:, wa:] = acc[:out_rows]

    for copy in started:
        copy.wait_send()


def on_device(
    nz, nx, teacher_in, norm_gain, gate_w, up_w, down_w, prev_rows, student_in, student_w, target_rows, counts
):
    nk = NY * nx
    ndp = nk * nz
    ntok, nfeat = teacher_in.shape
    trows, width = prev_rows.shape
    s_dev, ds = student_in.shape
    groups = lax.axis_size("grp")
    cap_z = nz * CAP
    part = ds // nk
    out_rows = part // nz
    d_model = ndp * nfeat
    wa = width - width // 4
    vm = pl.BlockSpec(memory_space=pltpu.VMEM)
    hbm = pl.BlockSpec(memory_space=pl.ANY)
    sm = pl.BlockSpec(memory_space=pltpu.SMEM)
    v = pltpu.VMEM
    scratch = [
        v((2 * nfeat, d_model), BF16),
        v((nfeat, d_model), BF16),
        v((nk, nz, CAP, ds), BF16),
        v((ds, width), BF16),
        v((nk, CAP, ndp), jnp.int32),
        v((nz, nk, FA, ntok), BF16),
        v((nk, nz, nfeat - FA, ntok), BF16),
        v((NY * nz, nx, nfeat, ntok), BF16),
        v((8, ntok), F32),
        v((8, ntok), F32),
        v((nz, 8, ntok), F32),
        v((nk, 8, ntok), F32),
        v((2, nz, trows, width // 2), BF16),
        v((nk, nz * trows, cap_z), BF16),
        v((2, nk, width // 2, cap_z), BF16),
        v((2, nk, width // 2, cap_z), BF16),
        v((width, ds), BF16),
        v((ds, s_dev), BF16),
        v((nk, width, cap_z), F32),
        v((3, nk, cap_z), F32),
        v((groups, 3, nk, cap_z), F32),
        v((width, s_dev), BF16),
        v((part, wa), F32),
        v((nk, part, wa), BF16),
        v((nk, part, wa), BF16),
        v((part + 16, wa), F32),
        v((nz, 16, wa), BF16),
        v((nz, 16, wa), BF16),
        v((ds + 16, width - wa), F32),
        v((nz, nk, 16, width - wa), BF16),
        v((nz, nk, 16, width - wa), BF16),
        v((nk, 16, width - wa), BF16),
        v((nk, 16, width - wa), BF16),
        v((nk, cap_z), F32),
        v((nk, cap_z), F32),
        v((nk, nk, cap_z), F32),
        v((nz, nk, cap_z), F32),
        v((NY * nz, nx, nfeat, ntok), F32),
        v((nk, nz, MA, ntok), BF16),
        v((nz, nk, nfeat - MA, ntok), BF16),
        v((nk, nz, MA, ntok), BF16),
        v((nz, nk, nfeat - MA, ntok), BF16),
        v((nz, MA, ntok), F32),
        v((nk, nfeat - MA, ntok), F32),
        v((nz, MA, ntok), BF16),
        v((nk, nfeat - MA, ntok), BF16),
        v((nz, MA, ntok), BF16),
        v((nk, nfeat - MA, ntok), BF16),
        pltpu.SemaphoreType.DMA((STAGES, max(nk, nz, groups))),
        pltpu.SemaphoreType.DMA((STAGES, max(nk, nz, groups))),
        pltpu.SemaphoreType.DMA((NY + 4 + nk,)),
    ]
    tout, gout, loss = pl.pallas_call(
        functools.partial(kernel, nz, nx),
        out_shape=(
            jax.ShapeDtypeStruct((nfeat, ntok), BF16),
            jax.ShapeDtypeStruct((out_rows, width), F32),
            jax.ShapeDtypeStruct((1, 1), F32),
        ),
        in_specs=[vm, vm, vm, hbm, hbm, hbm, hbm, hbm, hbm, sm],
        out_specs=(vm, vm, sm),
        scratch_shapes=scratch,
        compiler_params=pltpu.CompilerParams(
            collective_id=0, has_side_effects=True, vmem_limit_bytes=60 * 1024 * 1024
        ),
        name="distill",
    )(
        teacher_in.T,
        norm_gain.reshape(1, nfeat),
        prev_rows,
        gate_w.T,
        up_w.T,
        down_w,
        student_in.reshape(NY, nz, nx, CAP, ds),
        student_w,
        target_rows.transpose(0, 2, 1).reshape(NY, nz, nx, CAP, ndp),
        counts,
    )
    return tout.T, gout, loss.reshape(())


def solution(mesh):
    in_specs = (
        P("grp", "dp"),
        P("dp"),
        P(None, "dp"),
        P(None, "dp"),
        P("dp", None),
        P("dp", "grp"),
        P("dp", None),
        P(None, "grp"),
        P(),
        P(),
    )
    out_specs = (P("grp", "dp"), P("dp", "grp"), P())
    nx = 4
    nz = mesh.shape["dp"] // (NY * nx)
    return jax.shard_map(
        functools.partial(on_device, nz, nx), mesh=mesh, in_specs=in_specs, out_specs=out_specs, check_vma=False
    )
```
